32 devices in a mesh: row: 2 (over core), col: 8 (over z, y), layer: 2 (over x).
Axes of the slice: x: 2, y: 2, z: 4, core: 2. Of those that a mesh axis runs over, the one named last changes fastest.
Arguments:
- u_values: float32 [64, 4, 2, 128, 128], P(('row', 'col'), None, 'layer'), may hold values from -0.1875 to 0.1875
- u_mask: int32 [64, 4, 2], P(('row', 'col'), None, 'layer'), may hold values 0 or 1
- p_values: float32 [32, 2, 8, 128, 128], P(('row', 'col'), 'layer'), may hold values from -6 to 6
- p_mask: int32 [32, 2, 8], P(('row', 'col'), 'layer'), may hold values 0 or 1
- t_mask: int32 [64, 4, 2], P(('row', 'col'), None, 'layer'), may hold values 0 or 1
- out_mask: int32 [32, 2, 8], P(('row', 'col'), 'layer'), may hold values 0 or 1
Outputs:
- new_density: float32 [32, 2, 8, 128, 128], P(('row', 'col'), 'layer')
The draws below stay inside these ranges and needn't reach their ends.
All inputs are finite; a program needn't handle non-finite values. No bound on the sum of `u_mask` or of `p_mask` or of `t_mask` or of `out_mask` on one device may be relied on, other than what follows from the above.
Results may differ from the reference program's by a relative error of at most 0.0001.
Values sent between devices are 32-bit elements; how exact they have to be, the bound alone decides.
No kernel may reach another device: no remote copies, remote signals or barrier semaphores. Data moves between devices by JAX's collectives and lax.ppermute only.
A program may use at most 64 MiB of HBM per device.

```python
import jax
import jax.numpy as jnp
from jax import lax

BLK = 128
NO = 8
REACH = 4
NB = 64
N_LAYER = 2


def set_ends(values, rng, least, high):
    extent = values.shape
    spot = [jax.random.randint(jax.random.fold_in(rng, axis), (), 0, extent[axis]) for axis in range(len(extent))]
    values = values.at[tuple(spot)].set(least)
    longest = extent.index(max(extent))
    spot[longest] = (spot[longest] + 1) % extent[longest]
    return values.at[tuple(spot)].set(high)


def levels(stream_key, dims, split, low, high):
    factor_of = 1.0
    for axis_at, shards_of in split:
        draws = jax.random.uniform(jax.random.fold_in(jax.random.fold_in(stream_key, 6), axis_at), (shards_of,), jnp.float32, low / len(split), high / len(split))
        factor_of = factor_of * jnp.repeat(jnp.exp(draws), dims[axis_at] // shards_of).reshape((-1,) + (1,) * (len(dims) - 1 - axis_at))
    return factor_of


def bell_draw(key, shape, deviation, reach, split=(), held_as=jnp.bfloat16):
    entries = jax.random.normal(key, shape, jnp.float32) * deviation
    if len(split) > 0:
        entries = levels(key, shape, split, -0.22, 0.18) * entries
    return jnp.clip(entries, min=-reach, max=reach).astype(held_as)


def setup_inputs(seed: int = 0) -> dict:
    seeds = jax.random.split(jax.random.key(seed), 7)
    return {
        "u_values": bell_draw(seeds[0], (NB, NO // N_LAYER, N_LAYER, BLK, BLK), (NO * BLK) ** -0.5, 0.1875, ((0, 16), (2, 2)), jnp.float32),
        "u_mask": set_ends((jax.random.randint(seeds[1], (NB, NO // N_LAYER, N_LAYER), 0, 5) < 3).astype(jnp.int32), jax.random.fold_in(seeds[1], 1), 0, 1),
        "p_values": bell_draw(seeds[2], (NB // N_LAYER, N_LAYER, NO, BLK, BLK), 1.0, 6.0, ((0, 16), (1, 2)), jnp.float32),
        "p_mask": set_ends((jax.random.randint(seeds[3], (NB // N_LAYER, N_LAYER, NO), 0, 5) < 3).astype(jnp.int32), jax.random.fold_in(seeds[3], 1), 0, 1),
        "t_mask": set_ends((jax.random.randint(seeds[4], (NB, NO // N_LAYER, N_LAYER), 0, 5) < 3).astype(jnp.int32), jax.random.fold_in(seeds[4], 1), 0, 1),
        "out_mask": set_ends((jax.random.randint(seeds[5], (NB // N_LAYER, N_LAYER, NO), 0, 5) < 3).astype(jnp.int32), jax.random.fold_in(seeds[5], 1), 0, 1),
    }


def class_to_offset(source):
    parted = source.reshape((NB // N_LAYER, N_LAYER) + source.shape[1:])
    rolled = [jnp.roll(parted[:, r], -r, axis=2) for r in range(N_LAYER)]
    stacked = jnp.stack(rolled, axis=1)
    return stacked.reshape((NB, NO) + source.shape[3:])


def band_valid():
    row_index = jnp.arange(NB, dtype=jnp.int32)[:, None]
    offsets = jnp.arange(NO, dtype=jnp.int32)[None, :]
    column = row_index - REACH + offsets
    return ((column >= 0) & (column < NB)).astype(jnp.float32)


def reference(u_values, u_mask, p_values, p_mask, t_mask, out_mask):
    valid = band_valid()
    u_keep = class_to_offset(u_mask).astype(jnp.float32) * valid
    u_band = class_to_offset(u_values) * u_keep[:, :, None, None]
    p_keep = p_mask.reshape(NB, NO).astype(jnp.float32) * valid
    p_band = p_values.reshape(NB, NO, BLK, BLK) * p_keep[:, :, None, None]
    p_padded = jnp.pad(p_band, ((REACH, REACH), (0, 0), (0, 0), (0, 0)))
    product = jnp.zeros((NB, NO, BLK, BLK), jnp.float32)
    for ou in range(NO):
        low = max(0, REACH - ou)
        high = min(NO, NO + REACH - ou)
        p_rows = p_padded[ou:ou + NB, low:high]
        term = jnp.einsum("iab,iobc->ioac", u_band[:, ou], p_rows, precision=lax.Precision.HIGHEST)
        product = product.at[:, ou + low - REACH:ou + high - REACH].add(term)
    t_keep = class_to_offset(t_mask).astype(jnp.float32) * valid
    product = product * t_keep[:, :, None, None]
    u_padded = jnp.pad(u_band, ((REACH, REACH), (0, 0), (0, 0), (0, 0)))
    columns = []
    for op in range(NO):
        low = max(0, op - REACH)
        high = min(NO, NO + op - REACH)
        u_rows = u_padded[op:op + NB, low - op + REACH:high - op + REACH]
        columns.append(jnp.einsum("ioab,iocb->iac", product[:, low:high], u_rows, precision=lax.Precision.HIGHEST))
    result = jnp.stack(columns, axis=1)
    o_keep = out_mask.reshape(NB, NO).astype(jnp.float32) * valid
    result = result * o_keep[:, :, None, None]
    return result.reshape(NB // N_LAYER, N_LAYER, NO, BLK, BLK)
```

```python
import functools

import jax
import jax.numpy as jnp
from jax import lax
from jax.experimental import pallas as pl
from jax.experimental.pallas import tpu as pltpu
from jax.sharding import PartitionSpec as P

SLABS = ("row", "col")
F32 = jnp.float32
BF16 = jnp.bfloat16
VMEM = pl.BlockSpec(memory_space=pltpu.VMEM)
SMEM = pl.BlockSpec(memory_space=pltpu.SMEM)


def shape(*dims, dtype=F32):
    return jax.ShapeDtypeStruct(dims, dtype)


def call(body, outs, n_vmem, n_smem, scratch=(), flops=0):
    return pl.pallas_call(
        body,
        out_shape=outs,
        in_specs=[SMEM] * n_smem + [VMEM] * n_vmem,
        out_specs=[VMEM] * len(outs),
        scratch_shapes=list(scratch),
        cost_estimate=pl.CostEstimate(flops=flops, bytes_accessed=2 << 20, transcendentals=0),
        compiler_params=pltpu.CompilerParams(vmem_limit_bytes=40 << 20),
    )


def halves(x):
    high = x.astype(BF16)
    return high, (x - high.astype(F32)).astype(BF16)


def dot3(a, b, rhs_contract):
    one = functools.partial(
        lax.dot_general,
        dimension_numbers=(((1,), (rhs_contract,)), ((), ())),
        preferred_element_type=F32,
    )
    return one(a[0], b[0]) + (one(a[0], b[1]) + one(a[1], b[0]))


def aligned(block, size):
    return pl.multiple_of(block * size, size)


def keep_p(total_rows, where, p_mask, p, *outs):
    slab, layer = where[0], where[1]
    for a in range(2):
        row = slab * 4 + 2 * a + layer
        for o in range(8):
            col = row - 4 + o
            inside = (col >= 0) & (col < total_rows)
            keep = jnp.where(inside, p_mask[a, 0, o], 0).astype(F32)
            outs[2 * (o % 2) + a][o // 2] = p[a, 0, o] * keep


def keep_u(u_mask, u, *outs):
    for i in range(4):
        for m in range(4):
            outs[i][m] = u[i, m, 0] * u_mask[i, m, 0].astype(F32)


def slot_base(i, layer):
    return i // 2 if i % 2 == 0 else (i + 1) // 2 - layer


def product_t(size, where, t_mask, *refs):
    u_own, u_oth = refs[0:4], refs[4:8]
    pe, pc = refs[8:10], refs[10:12]
    pe_y, pc_y = refs[12:14], refs[14:16]
    pe_z, pc_z = refs[16:18], refs[18:20]
    t_hi, t_lo, ss = refs[20:23]
    own_hi, own_lo, oth_hi, oth_lo, ud_hi, ud_lo = refs[23:29]
    even, layer = where[0] % 2 == 0, where[1]
    for ref in (own_hi, own_lo, oth_hi, oth_lo, ud_hi, ud_lo):
        ref[...] = jnp.zeros_like(ref)
    for mine, other_y, other_z, hi_ref, lo_ref, shift in (
        (pe, pe_y, pe_z, own_hi, own_lo, -2),
        (pc, pc_y, pc_z, oth_hi, oth_lo, -1),
    ):
        for a in range(6):
            for e in range(4):
                c = a + e + shift
                if not 0 <= c < 6:
                    continue
                if a < 2:
                    block = jnp.where(even, other_z[a][e], other_y[a][e])
                elif a < 4:
                    block = mine[a - 2][e]
                else:
                    block = jnp.where(even, other_y[a - 4][e], other_z[a - 4][e])
                hi, lo = halves(block)
                at = (pl.ds(a * size, size), pl.ds(c * size, size))
                hi_ref[at], lo_ref[at] = hi, lo
    for i in range(4):
        left = [jnp.concatenate(x, axis=1) for x in zip(*[halves(u_own[i][m]) for m in range(4)])]
        other = [jnp.concatenate(x, axis=1) for x in zip(*[halves(u_oth[i][m]) for m in range(4)])]
        base = slot_base(i, layer)
        ud_hi[pl.ds(i * size, size), pl.ds(aligned(base, size), 4 * size)] = left[0]
        ud_lo[pl.ds(i * size, size), pl.ds(aligned(base, size), 4 * size)] = left[1]
        rows = pl.ds(aligned(base, size), 4 * size)
        band = (own_hi[rows, rows], own_lo[rows, rows])
        total = dot3(left, band, 0)
        rows = pl.ds(aligned(slot_base(i, 1 - layer), size), 4 * size)
        cols = pl.ds(aligned(i // 2 + layer if i % 2 == 0 else (i + 1) // 2, size), 4 * size)
        band = (oth_hi[rows, cols], oth_lo[rows, cols])
        total = total + dot3(other, band, 0)
        kept = jnp.concatenate(
            [total[:, m * size : (m + 1) * size] * t_mask[i, m, 0].astype(F32) for m in range(4)], axis=1
        )
        t_hi[i], t_lo[i] = halves(kept)
    for q in range(2):
        i = 2 * q + 1 - layer
        cols = pl.ds(aligned(q + 1 - layer, size), 4 * size)
        sums = dot3((t_hi[i], t_lo[i]), (ud_hi[:, cols], ud_lo[:, cols]), 1)
        for r in range(4):
            ss[q, r] = sums[:, r * size : (r + 1) * size]


def put_halo(size, even, layer, u_y, u_z, uh_hi, uh_lo):
    uh_hi[...] = jnp.zeros_like(uh_hi)
    uh_lo[...] = jnp.zeros_like(uh_lo)
    for at in range(7):
        if at < 4:
            base = slot_base(at, layer)
            pick = [jnp.where(even, u_z[at][m], u_y[at][m]) for m in range(4)]
        else:
            base = slot_base(at - 4, layer) + 4
            pick = [jnp.where(even, u_y[at - 4][m], u_z[at - 4][m]) for m in range(4)]
        both = [jnp.concatenate(x, axis=1) for x in zip(*[halves(x) for x in pick])]
        where = (pl.ds(at * size, size), pl.ds(aligned(base, size), 4 * size))
        uh_hi[where], uh_lo[where] = both


def halo_sums(size, i, base, t_hi, t_lo, uh_hi, uh_lo):
    cols = pl.ds(aligned(base + 2, size), 4 * size)
    rows = [pl.ds(aligned(jnp.where(t < i, 4 + t, t), size), size) for t in range(4)]
    hi = jnp.concatenate([uh_hi[r, cols] for r in rows], axis=0)
    lo = jnp.concatenate([uh_lo[r, cols] for r in rows], axis=0)
    return dot3((t_hi[i], t_lo[i]), (hi, lo), 1)


def send_halo(size, where, *refs):
    u_y, u_z = refs[0:4], refs[4:8]
    t_hi, t_lo, out, uh_hi, uh_lo = refs[8:13]
    layer = where[1]
    put_halo(size, where[0] % 2 == 0, layer, u_y, u_z, uh_hi, uh_lo)
    for q in range(2):
        sums = halo_sums(size, 2 * q + 1 - layer, q + 1 - layer, t_hi, t_lo, uh_hi, uh_lo)
        for t in range(4):
            out[q, t] = sums[:, t * size : (t + 1) * size]


def keep_rows(size, where, *refs):
    u_own, u_y, u_z = refs[0:4], refs[4:8], refs[8:12]
    t_hi, t_lo, out, uh_hi, uh_lo, ud_hi, ud_lo = refs[12:19]
    layer = where[1]
    put_halo(size, where[0] % 2 == 0, layer, u_y, u_z, uh_hi, uh_lo)
    ud_hi[...] = jnp.zeros_like(ud_hi)
    ud_lo[...] = jnp.zeros_like(ud_lo)
    for i in range(4):
        left = [jnp.concatenate(x, axis=1) for x in zip(*[halves(u_own[i][m]) for m in range(4)])]
        cols = pl.ds(aligned(slot_base(i, layer), size), 4 * size)
        ud_hi[pl.ds(i * size, size), cols] = left[0]
        ud_lo[pl.ds(i * size, size), cols] = left[1]
    for q in range(2):
        i = 2 * q + layer
        sums = halo_sums(size, i, q, t_hi, t_lo, uh_hi, uh_lo)
        for t in range(4):
            out[q, (8 - i + t) % 8] = sums[:, t * size : (t + 1) * size]
        cols = pl.ds(q * size, 4 * size)
        sums = dot3((t_hi[i], t_lo[i]), (ud_hi[:, cols], ud_lo[:, cols]), 1)
        for r in range(4):
            out[q, (4 - i + r) % 8] = sums[:, r * size : (r + 1) * size]


def combine(total_rows, where, o_mask, kept, ss, halo, out):
    slab, layer = where[0], where[1]
    for q in range(2):
        i = 2 * q + layer
        for t in range(8):
            o = (4 - i + t) % 8
            col = slab * 4 + i - 4 + o
            inside = (col >= 0) & (col < total_rows)
            keep = jnp.where(inside, o_mask[q, 0, o], 0).astype(F32)
            got = ss[q, t] if t < 4 else halo[q, t - 4]
            out[q, 0, o] = (kept[q, o] + got) * keep


def on_device(u_values, u_mask, p_values, p_mask, t_mask, out_mask):
    size = u_values.shape[-1]
    slabs = lax.axis_size(SLABS)
    total_rows = slabs * u_values.shape[0]
    where = jnp.stack([lax.axis_index(SLABS), lax.axis_index("layer")]).astype(jnp.int32)
    swap = [(0, 1), (1, 0)]
    pair = [(s, s ^ 1) for s in range(slabs)]
    onward = [(s, s + 2) for s in range(0, slabs - 2, 2)] + [(s, s - 2) for s in range(3, slabs, 2)]

    def over_layer(xs):
        return [lax.ppermute(x, "layer", swap) for x in xs]

    def over_pair(xs):
        return [lax.ppermute(x, SLABS, pair) for x in xs]

    def over_onward(xs):
        return [lax.ppermute(x, SLABS, onward) for x in xs]

    four = shape(4, size, size)
    wide = 6 * size
    pe0, pe1, po0, po1 = call(functools.partial(keep_p, total_rows), [four] * 4, 1, 2)(where, p_mask, p_values)
    pe = [pe0, pe1]
    pc = over_layer([po0, po1])
    pe_y = over_pair(pe)
    pe_z = over_onward(pe_y)
    u_own = call(keep_u, [four] * 4, 1, 1)(u_mask, u_values)
    u_oth = over_layer(u_own)
    pc_y = over_pair(pc)
    pc_z = over_onward(pc_y)
    late = lax.optimization_barrier((*u_own, pc[1]))[:4]
    u_y = over_pair(late)
    u_z = over_onward(u_y)
    t_hi, t_lo, ss = call(
        functools.partial(product_t, size),
        [shape(4, size, 4 * size, dtype=BF16)] * 2 + [shape(2, 4, size, size)],
        20,
        2,
        [pltpu.VMEM((wide, wide), BF16)] * 4 + [pltpu.VMEM((4 * size, wide), BF16)] * 2,
        flops=3 * (4 * 32 + 2 * 16) * 2 * size**3,
    )(where, t_mask, *u_own, *u_oth, *pe, *pc, *pe_y, *pc_y, *pe_z, *pc_z)
    ss_got = lax.ppermute(ss, "layer", swap)
    halo_scratch = [pltpu.VMEM((7 * size, 9 * size), BF16)] * 2
    (halo,) = call(
        functools.partial(send_halo, size),
        [shape(2, 4, size, size)],
        10,
        1,
        halo_scratch,
        flops=3 * 32 * 2 * size**3,
    )(where, *u_y, *u_z, t_hi, t_lo)
    halo_got = lax.ppermute(halo, "layer", swap)
    (kept,) = call(
        functools.partial(keep_rows, size),
        [shape(2, 8, size, size)],
        14,
        1,
        halo_scratch + [pltpu.VMEM((4 * size, wide), BF16)] * 2,
        flops=3 * 64 * 2 * size**3,
    )(where, *u_own, *u_y, *u_z, t_hi, t_lo)
    (out,) = call(functools.partial(combine, total_rows), [shape(2, 1, 8, size, size)], 3, 2)(
        where, out_mask, kept, ss_got, halo_got
    )
    return out


def solution(mesh):
    placed = (
        P(SLABS, None, "layer", None, None),
        P(SLABS, None, "layer"),
        P(SLABS, "layer", None, None, None),
        P(SLABS, "layer", None),
        P(SLABS, None, "layer"),
        P(SLABS, "layer", None),
    )
    return jax.shard_map(
        on_device,
        mesh=mesh,
        in_specs=placed,
        out_specs=P(SLABS, "layer", None, None, None),
        check_vma=False,
    )
```

```python
import functools

import jax
import jax.numpy as jnp
from jax import lax
from jax.experimental import pallas as pl
from jax.experimental.pallas import tpu as pltpu
from jax.sharding import PartitionSpec as P

SLABS = ("row", "col")
LIMIT = 63
F32 = jnp.float32
BF16 = jnp.bfloat16
VMEM = pl.BlockSpec(memory_space=pltpu.VMEM)
SMEM = pl.BlockSpec(memory_space=pltpu.SMEM)
ANY = pl.BlockSpec(memory_space=pl.ANY)

PACK = (
    [(0, 0), (0, 1), (0, 2), (0, 3), (1, 0), (1, 1), (1, 2), (2, 0), (2, 1), (2, 2), (1, 3), (2, 3)]
    + [(3, 0), (3, 1), (3, 2), (3, 3)],
    [(0, 2), (0, 3), (1, 1), (1, 2), (1, 3), (2, 1), (2, 2), (2, 3), (3, 0), (3, 1), (3, 2), (3, 3)]
    + [(0, 0), (0, 1), (1, 0), (2, 0)],
)
PIECES = (6, 6, 4)


def shape(*dims, dtype=F32):
    return jax.ShapeDtypeStruct(dims, dtype)


def call(body, outs, ins, scratch=(), flops=0, alias=None, out_spec=VMEM):
    return pl.pallas_call(
        body,
        out_shape=outs,
        in_specs=ins,
        out_specs=[out_spec] * len(outs),
        scratch_shapes=list(scratch),
        input_output_aliases=alias or {},
        cost_estimate=pl.CostEstimate(flops=flops, bytes_accessed=0, transcendentals=0),
        compiler_params=pltpu.CompilerParams(vmem_limit_bytes=LIMIT << 20),
    )


def halves(x):
    high = x.astype(BF16)
    return high, (x - high.astype(F32)).astype(BF16)


def dot3(a, b, rhs_contract):
    one = functools.partial(
        lax.dot_general,
        dimension_numbers=(((1,), (rhs_contract,)), ((), ())),
        preferred_element_type=F32,
    )
    return one(a[0], b[0]) + (one(a[0], b[1]) + one(a[1], b[0]))


def joined(blocks, axis):
    return [jnp.concatenate(x, axis=axis) for x in zip(*[halves(b) for b in blocks])]


def aligned(block, size):
    return pl.multiple_of(block * size, size)


def slot_base(i, layer):
    return i // 2 if i % 2 == 0 else (i + 1) // 2 - layer


def start(src, dst, sem):
    copy = pltpu.make_async_copy(src, dst, sem)
    copy.start()
    return copy


def keep_p(total_rows, where, p_mask_any, p_any, *refs):
    outs, (p_mask, p, sems) = refs[0:4], refs[4:]
    copies = [start(p_any.at[a], p.at[a], sems.at[a]) for a in range(2)]
    start(p_mask_any, p_mask, sems.at[2]).wait()
    slab, layer = where[0], where[1]
    for a in range(2):
        copies[a].wait()
        row = slab * 4 + 2 * a + layer
        for o in range(8):
            col = row - 4 + o
            inside = (col >= 0) & (col < total_rows)
            keep = jnp.where(inside, p_mask[a, 0, o], 0).astype(F32)
            outs[2 * (o % 2) + a][o // 2] = p[a, 0, o] * keep


def keep_u(where, u_mask, u_any, *refs):
    rows, packed, (u, sem) = refs[0], refs[1:4], refs[4:]
    start(u_any, u, sem).wait()
    even = where[0] % 2 == 0
    for i in range(4):
        for m in range(4):
            rows[i, m] = u[i, m, 0] * u_mask[i, m, 0].astype(F32)
    for par, case in ((0, even), (1, jnp.logical_not(even))):

        @pl.when(case)
        def _(par=par):
            for n, (r, m) in enumerate(PACK[par]):
                packed[n // 6][n % 6] = rows[r, m]


def fill_band(size, stage, hi_ref, lo_ref, shift, rows):
    for a in rows:
        for c in range(6):
            e = c - a - shift
            at = (pl.ds(a * size, size), pl.ds(c * size, size))
            if 0 <= e < 4:
                hi_ref[at], lo_ref[at] = halves(stage[a, e])
            else:
                hi_ref[at] = jnp.zeros((size, size), BF16)
                lo_ref[at] = jnp.zeros((size, size), BF16)


def gather_band(where, mine, other_y, other_z, stage, sems):
    even = where[0] % 2 == 0
    at_y, at_z = jnp.where(even, 4, 0), jnp.where(even, 0, 4)
    copies = []
    for a in range(2):
        copies.append(start(mine[a], stage.at[2 + a], sems.at[a]))
        copies.append(start(other_y[a], stage.at[at_y + a], sems.at[2 + a]))
        copies.append(start(other_z[a], stage.at[at_z + a], sems.at[4 + a]))
    return copies


def product_own(size, where, u_any, *refs):
    mine, other_y, other_z = refs[0:2], refs[2:4], refs[4:6]
    out, stage, u, hi, lo, sems = refs[6:]
    layer = where[1]
    copies = gather_band(where, mine, other_y, other_z, stage, sems)
    copy = start(u_any, u, sems.at[6])
    for c in copies:
        c.wait()
    fill_band(size, stage, hi, lo, -2, range(6))
    copy.wait()
    for i in range(4):
        left = joined([u[i, m] for m in range(4)], 1)
        rows = pl.ds(aligned(slot_base(i, layer), size), 4 * size)
        out[i] = dot3(left, (hi[rows, rows], lo[rows, rows]), 0)


def product_t(size, where, t_mask, u_any, t_own, u_cross, *refs):
    mine, other_y, other_z = refs[0:2], refs[2:4], refs[4:6]
    t_hi, t_lo, ss = refs[6:9]
    stage, u, u_oth, t_part, hi, lo, ud_hi, ud_lo, sems = refs[9:]
    layer = where[1]
    copies = gather_band(where, mine, other_y, other_z, stage, sems)
    u_copy = start(u_any, u, sems.at[6])
    t_copy = start(t_own, t_part, sems.at[7])
    x_copies = [start(u_cross.at[pl.ds(2 * h, 2)], u_oth.at[pl.ds(2 * h, 2)], sems.at[8 + h]) for h in range(2)]
    u_copy.wait()
    ud_hi[...] = jnp.zeros_like(ud_hi)
    ud_lo[...] = jnp.zeros_like(ud_lo)
    for i in range(4):
        cols = pl.ds(aligned(slot_base(i, layer), size), 4 * size)
        rows = pl.ds(i * size, size)
        blocks = [u[i, m] for m in range(4)]
        ud_hi[rows, cols], ud_lo[rows, cols] = joined(blocks, 1)
    for c in copies:
        c.wait()
    fill_band(size, stage, hi, lo, -1, range(6))
    t_copy.wait()
    for i in range(4):
        if i % 2 == 0:
            x_copies[i // 2].wait()
        other = joined([u_oth[i, m] for m in range(4)], 1)
        rows = pl.ds(aligned(slot_base(i, 1 - layer), size), 4 * size)
        cols = pl.ds(aligned(i // 2 + layer if i % 2 == 0 else (i + 1) // 2, size), 4 * size)
        total = t_part[i] + dot3(other, (hi[rows, cols], lo[rows, cols]), 0)
        kept = jnp.concatenate(
            [total[:, m * size : (m + 1) * size] * t_mask[i, m, 0].astype(F32) for m in range(4)], axis=1
        )
        t_hi[i], t_lo[i] = halves(kept)
    for q in range(2):
        i = 2 * q + 1 - layer
        cols = pl.ds(aligned(q + 1 - layer, size), 4 * size)
        sums = dot3((t_hi[i], t_lo[i]), (ud_hi[:, cols], ud_lo[:, cols]), 1)
        for r in range(4):
            ss[q, r] = sums[:, r * size : (r + 1) * size]


def gather_halo(u_y, u_z, stage, sems):
    spots = [stage.at[pl.ds(at, n)] for at, n in ((0, 6), (6, 6), (12, 4), (16, 6), (22, 6))]
    return [start(src, dst, sems.at[n]) for n, (src, dst) in enumerate(zip([*u_y, *u_z], spots))]


def fill_halo(size, where, stage, uh_hi, uh_lo):
    even, layer = where[0] % 2 == 0, where[1]
    uh_hi[...] = jnp.zeros_like(uh_hi)
    uh_lo[...] = jnp.zeros_like(uh_lo)
    for below_at, above_at, pack, case in ((16, 0, PACK[1], even), (0, 16, PACK[0], jnp.logical_not(even))):

        @pl.when(case)
        def _(below_at=below_at, above_at=above_at, pack=pack):
            for first, base, limit in ((below_at, 0, 4), (above_at, 4, 3)):
                for n, (r, m) in enumerate(pack[: 16 if first == 0 else 12]):
                    if r >= limit:
                        continue
                    rows = pl.ds((base + r) * size, size)
                    cols = pl.ds(aligned(slot_base(r, layer) + base + m, size), size)
                    uh_hi[rows, cols], uh_lo[rows, cols] = halves(stage[first + n])


def halo_sums(size, i, base, t_hi, t_lo, uh_hi, uh_lo):
    cols = pl.ds(aligned(base + 2, size), 4 * size)
    rows = [pl.ds(aligned(jnp.where(t < i, 4 + t, t), size), size) for t in range(4)]
    hi = jnp.concatenate([uh_hi[r, cols] for r in rows], axis=0)
    lo = jnp.concatenate([uh_lo[r, cols] for r in rows], axis=0)
    return dot3((t_hi[i], t_lo[i]), (hi, lo), 1)


def send_halo(size, where, *refs):
    u_y, u_z, t_any = refs[0:3], refs[3:5], refs[5:7]
    out, stage, t_hi, t_lo, uh_hi, uh_lo, sems = refs[7:]
    layer = where[1]
    copies = gather_halo(u_y, u_z, stage, sems)
    copies += [start(t_any[n], (t_hi, t_lo)[n], sems.at[7 + n]) for n in range(2)]
    for c in copies:
        c.wait()
    fill_halo(size, where, stage, uh_hi, uh_lo)
    for q in range(2):
        sums = halo_sums(size, 2 * q + 1 - layer, q + 1 - layer, t_hi, t_lo, uh_hi, uh_lo)
        for t in range(4):
            out[q, t] = sums[:, t * size : (t + 1) * size]


def out_keep(total_rows, where, o_mask, q, o):
    col = where[0] * 4 + 2 * q + where[1] - 4 + o
    return jnp.where((col >= 0) & (col < total_rows), o_mask[q, 0, o], 0).astype(F32)


def keep_rows(total_rows, size, where, o_mask, u_any, ss_any, *refs):
    u_y, u_z, t_any = refs[0:3], refs[3:5], refs[5:7]
    out, stage, u, ss, t_hi, t_lo, uh_hi, uh_lo, ud_hi, ud_lo, sems = refs[7:]
    layer = where[1]
    copies = gather_halo(u_y, u_z, stage, sems)
    copies += [start(t_any[n], (t_hi, t_lo)[n], sems.at[7 + n]) for n in range(2)]
    copies += [start(u_any, u, sems.at[9]), start(ss_any, ss, sems.at[10])]
    for c in copies:
        c.wait()
    fill_halo(size, where, stage, uh_hi, uh_lo)
    ud_hi[...] = jnp.zeros_like(ud_hi)
    ud_lo[...] = jnp.zeros_like(ud_lo)
    for i in range(4):
        cols = pl.ds(aligned(slot_base(i, layer), size), 4 * size)
        rows = pl.ds(i * size, size)
        blocks = [u[i, m] for m in range(4)]
        ud_hi[rows, cols], ud_lo[rows, cols] = joined(blocks, 1)
    for q in range(2):
        i = 2 * q + layer
        sums = halo_sums(size, i, q, t_hi, t_lo, uh_hi, uh_lo)
        for t in range(4):
            out[q, 0, (8 - i + t) % 8] = sums[:, t * size : (t + 1) * size]
        cols = pl.ds(q * size, 4 * size)
        sums = dot3((t_hi[i], t_lo[i]), (ud_hi[:, cols], ud_lo[:, cols]), 1)
        for r in range(4):
            o = (4 - i + r) % 8
            keep = out_keep(total_rows, where, o_mask, q, o)
            out[q, 0, o] = (sums[:, r * size : (r + 1) * size] + ss[q, r]) * keep


def combine(total_rows, where, o_mask, kept_any, halo_any, out_any, kept, halo, sems):
    layer = where[1]
    copies = []
    for q in range(2):
        i = 2 * q + layer
        first = start(halo_any.at[q], halo.at[q], sems.at[8 + q])
        rest = [start(kept_any.at[q, 0, (8 - i + t) % 8], kept.at[q, t], sems.at[4 * q + t]) for t in range(4)]
        copies.append((first, rest))
    stores = []
    for q in range(2):
        i = 2 * q + layer
        copies[q][0].wait()
        for t in range(4):
            o = (8 - i + t) % 8
            copies[q][1][t].wait()
            kept[q, t] = (kept[q, t] + halo[q, t]) * out_keep(total_rows, where, o_mask, q, o)
            stores.append(start(kept.at[q, t], out_any.at[q, 0, o], sems.at[10 + 4 * q + t]))
    for s in stores:
        s.wait()


def after(x, *others):
    return lax.optimization_barrier((x, *others))[0]


def on_device(u_values, u_mask, p_values, p_mask, t_mask, out_mask):
    size = u_values.shape[-1]
    slabs = lax.axis_size(SLABS)
    total_rows = slabs * u_values.shape[0]
    where = jnp.stack([lax.axis_index(SLABS), lax.axis_index("layer")]).astype(jnp.int32)
    swap = [(0, 1), (1, 0)]
    pair = [(s, s ^ 1) for s in range(slabs)]
    onward = [(s, s + 2) for s in range(0, slabs - 2, 2)] + [(s, s - 2) for s in range(3, slabs, 2)]

    def over_layer(x):
        return lax.ppermute(x, "layer", swap)

    def over_pair(x):
        return lax.ppermute(x, SLABS, pair)

    def onto(x):
        return lax.ppermute(x, SLABS, onward)

    def vmem(*dims, dtype=F32):
        return pltpu.VMEM(dims, dtype)

    def sems(n):
        return pltpu.SemaphoreType.DMA((n,))

    four = shape(4, size, size)
    six = shape(6, size, size)
    eight = shape(2, 4, size, size)
    sixteen = shape(4, 4, size, size)
    wide = 6 * size
    unit = 3 * 2 * (4 * size) ** 2 * size
    p_like = pltpu.VMEM(p_values.shape, F32)
    pe0, pe1, po0, po1 = call(
        functools.partial(keep_p, total_rows),
        [four] * 4,
        [SMEM, ANY, ANY],
        [pltpu.SMEM(p_mask.shape, jnp.int32), p_like, sems(3)],
    )(where, p_mask, p_values)
    pe = [pe0, pe1]
    pc = [over_layer(x) for x in (po0, po1)]
    pe_y = [over_pair(x) for x in pe]
    u_own, *packed = call(
        keep_u,
        [sixteen, six, six, four],
        [SMEM, SMEM, ANY],
        [pltpu.VMEM(u_values.shape, F32), pltpu.SemaphoreType.DMA],
    )(where, u_mask, u_values)
    u_oth = over_layer(after(u_own, pc[0]))
    pe_z = [onto(after(x, u_own)) for x in pe_y]
    pc_y = [over_pair(after(x, y)) for x, y in zip(pc, pe_y)]
    pc_z = [onto(after(x, z)) for x, z in zip(pc_y, pe_z)]
    band = [vmem(wide, wide, dtype=BF16)] * 2
    own_rows = [vmem(4 * size, wide, dtype=BF16)] * 2
    (t_own,) = call(
        functools.partial(product_own, size),
        [shape(4, size, 4 * size)],
        [SMEM] + [ANY] * 7,
        [vmem(6, 4, size, size), vmem(4, 4, size, size), *band, sems(7)],
        flops=4 * unit,
    )(where, u_own, *pe, *pe_y, *pe_z)
    u_y = [over_pair(after(x, pc[1], y)) for x, y in zip(packed[:2], pc_y)]
    u_y.append(over_pair(after(packed[2], u_y[0])))
    u_z = [onto(after(u_y[0], pc_z[0])), onto(after(u_y[1], pc_z[1], t_own))]
    t_hi, t_lo, ss = call(
        functools.partial(product_t, size),
        [shape(4, size, 4 * size, dtype=BF16)] * 2 + [eight],
        [SMEM] * 2 + [ANY] * 9,
        [vmem(6, 4, size, size)]
        + [vmem(4, 4, size, size)] * 2
        + [vmem(4, size, 4 * size), *band, *own_rows, sems(10)],
        flops=6 * unit,
    )(where, t_mask, u_own, t_own, u_oth, *pc, *pc_y, *pc_z)
    ss_got = over_layer(ss)
    halo_scratch = [vmem(7 * size, 9 * size, dtype=BF16)] * 2
    t_scratch = [vmem(4, size, 4 * size, dtype=BF16)] * 2
    (halo,) = call(
        functools.partial(send_halo, size),
        [eight],
        [SMEM] + [ANY] * 7,
        [vmem(28, size, size), *t_scratch, *halo_scratch, sems(9)],
        flops=2 * unit,
    )(where, *u_y, *u_z, t_hi, t_lo)
    halo_got = over_layer(halo)
    (kept,) = call(
        functools.partial(keep_rows, total_rows, size),
        [shape(*p_values.shape)],
        [SMEM] * 2 + [ANY] * 9,
        [vmem(28, size, size), vmem(4, 4, size, size), vmem(2, 4, size, size)]
        + [*t_scratch, *halo_scratch, *own_rows, sems(11)],
        flops=4 * unit,
    )(where, out_mask, u_own, ss_got, *u_y, *u_z, t_hi, t_lo)
    (out,) = call(
        functools.partial(combine, total_rows),
        [shape(*p_values.shape)],
        [SMEM, SMEM, ANY, ANY],
        [vmem(2, 4, size, size)] * 2 + [sems(18)],
        alias={2: 0},
        out_spec=ANY,
    )(where, out_mask, kept, halo_got)
    return out


def solution(mesh):
    placed = (
        P(SLABS, None, "layer", None, None),
        P(SLABS, None, "layer"),
        P(SLABS, "layer", None, None, None),
        P(SLABS, "layer", None),
        P(SLABS, None, "layer"),
        P(SLABS, "layer", None),
    )
    return jax.shard_map(
        on_device,
        mesh=mesh,
        in_specs=placed,
        out_specs=P(SLABS, "layer", None, None, None),
        check_vma=False,
    )
```

```python
import functools

import jax
import jax.numpy as jnp
from jax import lax
from jax.experimental import pallas as pl
from jax.experimental.pallas import tpu as pltpu
from jax.sharding import PartitionSpec as P

SLABS = ("row", "col")
F32 = jnp.float32
BF16 = jnp.bfloat16
VMEM = pl.BlockSpec(memory_space=pltpu.VMEM)
SMEM = pl.BlockSpec(memory_space=pltpu.SMEM)
ANY = pl.BlockSpec(memory_space=pl.ANY)
HBM = object()

PACK = (
    [(0, 0), (0, 1), (0, 2), (0, 3), (1, 0), (1, 1), (1, 2), (1, 3), (2, 0), (2, 1), (2, 2), (2, 3)]
    + [(3, 0), (3, 1), (3, 2), (3, 3)],
    [(0, 2), (0, 3), (1, 1), (1, 2), (1, 3), (2, 1), (2, 2), (2, 3), (3, 0), (3, 1), (3, 2), (3, 3)]
    + [(0, 0), (0, 1), (1, 0), (2, 0)],
)
PARTS = ((0, 7), (7, 9))


def shape(*dims, dtype=F32):
    return jax.ShapeDtypeStruct(dims, dtype)


def vmem(*dims, dtype=F32):
    return pltpu.VMEM(dims, dtype)


def call(body, outs, ins, scratch=(), flops=0, alias=None, limit=24):
    def run(*args):
        placed = [pltpu.with_memory_space_constraint(x, pltpu.HBM) if spec is HBM else x for spec, x in zip(ins, args)]
        return pl.pallas_call(
            body,
            out_shape=outs,
            in_specs=[ANY if spec is HBM else spec for spec in ins],
            out_specs=[ANY if isinstance(x, jax.ShapeDtypeStruct) else VMEM for x in outs],
            scratch_shapes=list(scratch),
            input_output_aliases=alias or {},
            cost_estimate=pl.CostEstimate(flops=flops, bytes_accessed=0, transcendentals=0),
            compiler_params=pltpu.CompilerParams(vmem_limit_bytes=limit << 20),
        )(*placed)

    return run


def halves(x):
    high = x.astype(BF16)
    return high, (x - high.astype(F32)).astype(BF16)


def dot3(a, b, rhs_contract):
    one = functools.partial(
        lax.dot_general,
        dimension_numbers=(((1,), (rhs_contract,)), ((), ())),
        preferred_element_type=F32,
    )
    return one(a[0], b[0]) + (one(a[0], b[1]) + one(a[1], b[0]))


def joined(blocks, axis):
    return [jnp.concatenate(x, axis=axis) for x in zip(*[halves(b) for b in blocks])]


def aligned(block, size):
    return pl.multiple_of(block * size, size)


def slot_base(i, layer):
    return i // 2 if i % 2 == 0 else (i + 1) // 2 - layer


def start(src, dst, sem):
    copy = pltpu.make_async_copy(src, dst, sem)
    copy.start()
    return copy


def keep_p(p_mask_any, p_any, *refs):
    outs, (p_mask, p, kept, sems) = refs[0:2], refs[2:]
    copies = [start(p_any.at[a], p.at[a], sems.at[a]) for a in range(2)]
    start(p_mask_any, p_mask, sems.at[2]).wait()
    stores = []
    for a in range(2):
        copies[a].wait()
        for r in (1, 0):
            for e in range(4):
                o = 2 * e + r
                kept[r, a, e] = p[a, 0, o] * p_mask[a, 0, o].astype(F32)
            stores.append(start(kept.at[r, a], outs[r].at[a], sems.at[3 + 2 * r + a]))
    for c in stores:
        c.wait()


def keep_u(where, u_mask_any, u_any, *refs):
    outs, (u_mask, u, rows, packed, sems) = refs[0:3], refs[3:]
    copies = [start(u_any.at[i], u.at[i], sems.at[i]) for i in range(4)]
    start(u_mask_any, u_mask, sems.at[4]).wait()
    even = where[0] % 2 == 0
    stores = []
    for i in range(4):
        copies[i].wait()
        for m in range(4):
            rows[i, m] = u[i, m, 0] * u_mask[i, m].astype(F32)
        stores.append(start(rows.at[i], outs[0].at[i], sems.at[5 + i]))
    for par, case in ((0, even), (1, jnp.logical_not(even))):

        @pl.when(case)
        def _(par=par):
            for n, block in enumerate(PACK[par]):
                packed[n] = rows[block]

    for n, (first, count) in enumerate(PARTS):
        stores.append(start(packed.at[pl.ds(first, count)], outs[1 + n], sems.at[9 + n]))
    for c in stores:
        c.wait()


def fill_band(size, stage, hi_ref, lo_ref, shift, rows):
    for a in rows:
        for c in range(6):
            e = c - a - shift
            at = (pl.ds(a * size, size), pl.ds(c * size, size))
            if 0 <= e < 4:
                hi_ref[at], lo_ref[at] = halves(stage[a, e])
            else:
                hi_ref[at] = jnp.zeros((size, size), BF16)
                lo_ref[at] = jnp.zeros((size, size), BF16)


def product_own(size, where, u_any, mine, other_y, other_z, t_own, ud_hi, ud_lo, stage, u, hi, lo, sems):
    even, layer = where[0] % 2 == 0, where[1]
    copies = [
        start(u_any, u, sems.at[0]),
        start(mine, stage.at[pl.ds(2, 2)], sems.at[1]),
        start(other_y, stage.at[pl.ds(jnp.where(even, 4, 0), 2)], sems.at[2]),
        start(other_z, stage.at[pl.ds(jnp.where(even, 0, 4), 2)], sems.at[3]),
    ]
    ud_hi[...] = jnp.zeros_like(ud_hi)
    ud_lo[...] = jnp.zeros_like(ud_lo)
    copies[0].wait()
    for i in range(4):
        cols = pl.ds(aligned(slot_base(i, layer), size), 4 * size)
        rows = pl.ds(i * size, size)
        ud_hi[rows, cols], ud_lo[rows, cols] = joined([u[i, m] for m in range(4)], 1)
    for c in copies[1:]:
        c.wait()
    fill_band(size, stage, hi, lo, -2, range(6))
    for i in range(4):
        cols = pl.ds(aligned(slot_base(i, layer), size), 4 * size)
        rows = pl.ds(i * size, size)
        t_own[i] = dot3((ud_hi[rows, cols], ud_lo[rows, cols]), (hi[cols, cols], lo[cols, cols]), 0)


def product_t(total_rows, size, where, t_mask_any, t_own, ud_hi, ud_lo, u_cross, *refs):
    sides, (t_hi, t_lo, ss) = refs[0:3], refs[3:6]
    t_mask, stage, u_oth, hi, lo, sems = refs[6:]
    slab, layer = where[0], where[1]
    even = slab % 2 == 0
    spots = (2, jnp.where(even, 4, 0), jnp.where(even, 0, 4))
    x_copy = start(u_cross, u_oth, sems.at[6])
    copies = [start(sides[n], stage.at[pl.ds(spots[n], 2)], sems.at[n]) for n in range(3)]
    mask_copy = start(t_mask_any, t_mask, sems.at[7])
    x_copy.wait()
    others = [joined([u_oth[i, m] for m in range(4)], 1) for i in range(4)]
    for c in copies:
        c.wait()
    mask_copy.wait()
    fill_band(size, stage, hi, lo, -1, range(6))
    for i in range(4):
        base = slot_base(i, layer)
        rows = pl.ds(aligned(slot_base(i, 1 - layer), size), 4 * size)
        cols = pl.ds(aligned(i // 2 + layer if i % 2 == 0 else (i + 1) // 2, size), 4 * size)
        total = t_own[i] + dot3(others[i], (hi[rows, cols], lo[rows, cols]), 0)
        kept = []
        for m in range(4):
            col = slab * 4 + 2 * (base + m) - 4 + layer
            keep = jnp.where((col >= 0) & (col < total_rows), t_mask[i, m], 0).astype(F32)
            kept.append(total[:, m * size : (m + 1) * size] * keep)
        t_hi[i], t_lo[i] = joined(kept, 1)
    for q in range(2):
        i = 2 * q + 1 - layer
        cols = pl.ds(aligned(q + 1 - layer, size), 4 * size)
        sums = dot3((t_hi[i], t_lo[i]), (ud_hi[:, cols], ud_lo[:, cols]), 1)
        for r in range(4):
            ss[q, r] = sums[:, r * size : (r + 1) * size]


def gather_halo(u_y, u_z, stage, sems):
    spots = [stage.at[pl.ds(at, n)] for at, n in (*PARTS, (16, 7), (23, 5))]
    return [start(src, spot, sems.at[n]) for n, (src, spot) in enumerate(zip([*u_y, *u_z], spots))]


def fill_halo(size, where, stage, uh_hi, uh_lo, rows=(0, 1, 2, 3)):
    even, layer = where[0] % 2 == 0, where[1]
    uh_hi[...] = jnp.zeros_like(uh_hi)
    uh_lo[...] = jnp.zeros_like(uh_lo)
    for below_at, above_at, pack, case in ((16, 0, PACK[1], even), (0, 16, PACK[0], jnp.logical_not(even))):

        @pl.when(case)
        def _(below_at=below_at, above_at=above_at, pack=pack):
            for first, above in ((below_at, 0), (above_at, 1)):
                for n, (r, m) in enumerate(pack[: 16 if first == 0 else 12]):
                    if r not in rows or (above and r == 3):
                        continue
                    at = pl.ds((above * len(rows) + rows.index(r)) * size, size)
                    cols = pl.ds(aligned(slot_base(r, layer) + 4 * above + m, size), size)
                    uh_hi[at, cols], uh_lo[at, cols] = halves(stage[first + n])


def halo_sums(size, i, base, t_rows, uh_hi, uh_lo, ts=(0, 1, 2, 3)):
    cols = pl.ds(aligned(base + 2, size), 4 * size)
    rows = [pl.ds(aligned(jnp.where(t < i, len(ts) + n, n), size), size) for n, t in enumerate(ts)]
    hi = jnp.concatenate([uh_hi[r, cols] for r in rows], axis=0)
    lo = jnp.concatenate([uh_lo[r, cols] for r in rows], axis=0)
    return dot3(t_rows, (hi, lo), 1)


def send_halo(size, ts, where, *refs):
    u_y, u_z, t_any = refs[0:2], refs[2:-9], refs[-9:-7]
    out, stage, t_hi, t_lo, uh_hi, uh_lo, sems = refs[-7:]
    layer = where[1]
    copies = gather_halo(u_y, u_z, stage, sems)
    for q in range(2):
        for n in range(2):
            copies.append(start(t_any[n].at[2 * q + 1 - layer], (t_hi, t_lo)[n].at[q], sems.at[5 + 2 * q + n]))
    for c in copies:
        c.wait()
    fill_halo(size, where, stage, uh_hi, uh_lo, ts)
    for q in range(2):
        sums = halo_sums(size, 2 * q + 1 - layer, q + 1 - layer, (t_hi[q], t_lo[q]), uh_hi, uh_lo, ts)
        for n in range(len(ts)):
            out[q, n] = sums[:, n * size : (n + 1) * size]


def out_keep(total_rows, where, o_mask, q, o):
    col = where[0] * 4 + 2 * q + where[1] - 4 + o
    return jnp.where((col >= 0) & (col < total_rows), o_mask[q, 0, o], 0).astype(F32)


def keep_rows(total_rows, size, where, o_mask, u_any, ss_any, *refs):
    u_y, u_z, t_any = refs[0:2], refs[2:4], refs[4:6]
    out_any, part, out, stage, u, ss, t_hi, t_lo, uh_hi, uh_lo, ud_hi, ud_lo, sems = refs[6:]
    layer = where[1]
    copies = gather_halo(u_y, u_z, stage, sems)
    copies += [start(t_any[n], (t_hi, t_lo)[n], sems.at[7 + n]) for n in range(2)]
    copies += [start(u_any, u, sems.at[9]), start(ss_any, ss, sems.at[10])]
    for c in copies:
        c.wait()
    fill_halo(size, where, stage, uh_hi, uh_lo)
    ud_hi[...] = jnp.zeros_like(ud_hi)
    ud_lo[...] = jnp.zeros_like(ud_lo)
    for i in range(4):
        cols = pl.ds(aligned(slot_base(i, layer), size), 4 * size)
        rows = pl.ds(i * size, size)
        ud_hi[rows, cols], ud_lo[rows, cols] = joined([u[i, m] for m in range(4)], 1)
    stores = []
    for q in range(2):
        i = 2 * q + layer
        sums = halo_sums(size, i, q, (t_hi[i], t_lo[i]), uh_hi, uh_lo)
        for t in range(4):
            o = (8 - i + t) % 8
            part[q, t] = sums[:, t * size : (t + 1) * size] * out_keep(total_rows, where, o_mask, q, o)
        cols = pl.ds(q * size, 4 * size)
        sums = dot3((t_hi[i], t_lo[i]), (ud_hi[:, cols], ud_lo[:, cols]), 1)
        for r in range(4):
            o = (4 - i + r) % 8
            keep = out_keep(total_rows, where, o_mask, q, o)
            out[q, r] = (sums[:, r * size : (r + 1) * size] + ss[q, r]) * keep
            stores.append(start(out.at[q, r], out_any.at[q, 0, o], sems.at[11 + 4 * q + r]))
    for c in stores:
        c.wait()


def combine(total_rows, where, o_mask, part, halo0, halo1, kept_any, out_any, done, sems):
    stores = []
    for q in range(2):
        for t in range(4):
            o = (8 - 2 * q - where[1] + t) % 8
            done[q, t] = part[q, t] + (halo0, halo1)[t // 2][q, t % 2] * out_keep(total_rows, where, o_mask, q, o)
            stores.append(start(done.at[q, t], out_any.at[q, 0, o], sems.at[4 * q + t]))
    for s in stores:
        s.wait()


def after(x, *others):
    return lax.optimization_barrier((x, *others))[0]


def on_device(u_values, u_mask, p_values, p_mask, t_mask, out_mask):
    size = u_values.shape[-1]
    slabs = lax.axis_size(SLABS)
    total_rows = slabs * u_values.shape[0]
    where = jnp.stack([lax.axis_index(SLABS), lax.axis_index("layer")]).astype(jnp.int32)
    swap = [(0, 1), (1, 0)]
    pair = [(s, s ^ 1) for s in range(slabs)]
    onward = [(s, s + 2) for s in range(0, slabs - 2, 2)] + [(s, s - 2) for s in range(3, slabs, 2)]

    def over_layer(x):
        return lax.ppermute(x, "layer", swap)

    def over_pair(x):
        return lax.ppermute(x, SLABS, pair)

    def onto(x):
        return lax.ppermute(x, SLABS, onward)

    def sems(n):
        return pltpu.SemaphoreType.DMA((n,))

    eight = shape(2, 4, size, size)
    wide = 6 * size
    unit = 3 * 2 * (4 * size) ** 2 * size
    pe, po = call(
        keep_p,
        [eight, eight],
        [HBM, HBM],
        [pltpu.SMEM(p_mask.shape, jnp.int32), vmem(*p_values.shape), vmem(2, 2, 4, size, size), sems(7)],
    )(p_mask, p_values)
    pc = over_layer(po)
    pe_y = over_pair(pe)
    u_mask, t_mask = u_mask[:, :, 0], t_mask[:, :, 0]
    u_own, *packed = call(
        keep_u,
        [shape(4, 4, size, size)] + [shape(n, size, size) for _, n in PARTS],
        [SMEM, HBM, HBM],
        [pltpu.SMEM(u_mask.shape, jnp.int32), vmem(*u_values.shape), vmem(4, 4, size, size)]
        + [vmem(16, size, size), sems(11)],
    )(where, u_mask, u_values)
    u_oth = over_layer(after(u_own, pc))
    pe_z = onto(after(pe_y, u_own))
    pc_y = over_pair(pc)
    pc_z = onto(pc_y)
    t_like = (4, size, 4 * size)
    band = [vmem(wide, wide, dtype=BF16)] * 2
    own_rows = [vmem(4 * size, wide, dtype=BF16)] * 2
    t_own, ud_hi, ud_lo = call(
        functools.partial(product_own, size),
        [vmem(*t_like), *own_rows],
        [SMEM] + [HBM] * 4,
        [vmem(6, 4, size, size), vmem(4, 4, size, size), *band, sems(4)],
        flops=4 * unit,
    )(where, u_own, pe, pe_y, pe_z)
    u_y = [over_pair(after(x, pc)) for x in packed]
    u_z = [onto(after(u_y[0], t_own))]
    t_hi, t_lo, ss = call(
        functools.partial(product_t, total_rows, size),
        [vmem(*t_like, dtype=BF16)] * 2 + [vmem(2, 4, size, size)],
        [SMEM, HBM, VMEM, VMEM, VMEM] + [HBM] * 4,
        [pltpu.SMEM(t_mask.shape, jnp.int32), vmem(6, 4, size, size), vmem(4, 4, size, size), *band, sems(8)],
        flops=6 * unit,
    )(where, after(t_mask, u_y[0]), t_own, ud_hi, ud_lo, u_oth, pc, pc_y, pc_z)
    ss_got = over_layer(ss)
    u_z.append(onto(after(u_y[1][:5], t_hi)))
    halos = []
    for ts in ((0, 1), (2, 3)):
        nz = 1 if ts[0] == 0 else 2
        (halo,) = call(
            functools.partial(send_halo, size, ts),
            [vmem(2, 2, size, size)],
            [SMEM] + [HBM] * (2 + nz) + [ANY] * 2,
            [vmem(28, size, size)]
            + [vmem(2, size, 4 * size, dtype=BF16)] * 2
            + [vmem(4 * size, 9 * size, dtype=BF16)] * 2
            + [sems(9)],
            flops=unit,
        )(where, *u_y, *u_z[:nz], t_hi, t_lo)
        t_lo = after(t_lo, halo)
        halos.append(over_layer(after(halo, *halos)))
    halo_scratch = [vmem(8 * size, 9 * size, dtype=BF16)] * 2
    t_scratch = [vmem(*t_like, dtype=BF16)] * 2
    kept, part = call(
        functools.partial(keep_rows, total_rows, size),
        [shape(*p_values.shape), vmem(2, 4, size, size)],
        [SMEM] * 2 + [HBM] * 6 + [ANY] * 2,
        [vmem(2, 4, size, size), vmem(28, size, size), vmem(4, 4, size, size), vmem(2, 4, size, size)]
        + [*t_scratch, *halo_scratch, *own_rows, sems(19)],
        flops=40 * unit,
    )(where, out_mask, u_own, ss_got, *u_y, *u_z, t_hi, t_lo)
    (out,) = call(
        functools.partial(combine, total_rows),
        [shape(*p_values.shape)],
        [SMEM, SMEM, VMEM, VMEM, VMEM, ANY],
        [vmem(2, 4, size, size), sems(8)],
        alias={5: 0},
        limit=16,
    )(where, out_mask, part, *halos, kept)
    return out


def solution(mesh):
    placed = (
        P(SLABS, None, "layer", None, None),
        P(SLABS, None, "layer"),
        P(SLABS, "layer", None, None, None),
        P(SLABS, "layer", None),
        P(SLABS, None, "layer"),
        P(SLABS, "layer", None),
    )
    return jax.shard_map(
        on_device,
        mesh=mesh,
        in_specs=placed,
        out_specs=P(SLABS, "layer", None, None, None),
        check_vma=False,
    )
```

```python
import functools

import jax
import jax.numpy as jnp
from jax import lax
from jax.experimental import pallas as pl
from jax.experimental.pallas import tpu as pltpu
from jax.sharding import PartitionSpec as P

SLABS = ("row", "col")
F32 = jnp.float32
BF16 = jnp.bfloat16
VMEM = pl.BlockSpec(memory_space=pltpu.VMEM)
SMEM = pl.BlockSpec(memory_space=pltpu.SMEM)
ANY = pl.BlockSpec(memory_space=pl.ANY)
HBM = object()

PACK = (
    [(0, 0), (0, 1), (0, 2), (0, 3), (1, 0), (1, 1), (1, 2), (1, 3), (2, 0), (2, 1), (2, 2), (2, 3)]
    + [(3, 0), (3, 1), (3, 2), (3, 3)],
    [(0, 2), (0, 3), (1, 1), (1, 2), (1, 3), (2, 1), (2, 2), (2, 3), (3, 0), (3, 1), (3, 2), (3, 3)]
    + [(0, 0), (0, 1), (1, 0), (2, 0)],
)
PARTS = ((0, 7), (7, 9))


def shape(*dims, dtype=F32):
    return jax.ShapeDtypeStruct(dims, dtype)


def vmem(*dims, dtype=F32):
    return pltpu.VMEM(dims, dtype)


def call(body, outs, ins, scratch=(), flops=0, alias=None, limit=24):
    def kernel(*refs):
        slab = lax.axis_index("row") * lax.axis_size("col") + lax.axis_index("col")
        body((slab, lax.axis_index("layer")), *refs)

    def run(*args):
        placed = [pltpu.with_memory_space_constraint(x, pltpu.HBM) if spec is HBM else x for spec, x in zip(ins, args)]
        return pl.pallas_call(
            kernel,
            out_shape=outs,
            in_specs=[ANY if spec is HBM else spec for spec in ins],
            out_specs=[ANY if isinstance(x, jax.ShapeDtypeStruct) else VMEM for x in outs],
            scratch_shapes=list(scratch),
            input_output_aliases=alias or {},
            cost_estimate=pl.CostEstimate(flops=flops, bytes_accessed=0, transcendentals=0),
            compiler_params=pltpu.CompilerParams(vmem_limit_bytes=limit << 20),
        )(*placed)

    return run


def halves(x):
    high = x.astype(BF16)
    return high, (x - high.astype(F32)).astype(BF16)


def dot3(a, b, rhs_contract):
    one = functools.partial(
        lax.dot_general,
        dimension_numbers=(((1,), (rhs_contract,)), ((), ())),
        preferred_element_type=F32,
    )
    return one(a[0], b[0]) + (one(a[0], b[1]) + one(a[1], b[0]))


def joined(blocks, axis):
    return [jnp.concatenate(x, axis=axis) for x in zip(*[halves(b) for b in blocks])]


def aligned(block, size):
    return pl.multiple_of(block * size, size)


def slot_base(i, layer):
    return i // 2 if i % 2 == 0 else (i + 1) // 2 - layer


def start(src, dst, sem):
    copy = pltpu.make_async_copy(src, dst, sem)
    copy.start()
    return copy


def keep_p(where, p_mask_any, p_any, *refs):
    outs, (p_mask, p, sems) = refs[0:2], refs[2:]
    even = where[0] % 2 == 0
    copies = [start(p_any.at[a], p.at[a], sems.at[a]) for a in range(2)]
    start(p_mask_any, p_mask, sems.at[2]).wait()
    for a in range(2):
        copies[a].wait()
        for o in range(8):
            n = 4 * a + o // 2
            outs[1 - o % 2][jnp.where(even, n, (n + 7) % 8)] = p[a, 0, o] * p_mask[a, 0, o].astype(F32)


def keep_u(where, u_mask_any, u_any, *refs):
    outs, (u_mask, u, rows, packed, sems) = refs[0:3], refs[3:]
    copies = [start(u_any.at[i], u.at[i], sems.at[i]) for i in range(4)]
    start(u_mask_any, u_mask, sems.at[4]).wait()
    even = where[0] % 2 == 0
    stores = []
    for i in range(4):
        copies[i].wait()
        for m in range(4):
            rows[i, m] = u[i, m, 0] * u_mask[i, m].astype(F32)
        stores.append(start(rows.at[i], outs[0].at[i], sems.at[5 + i]))
    for par, case in ((0, even), (1, jnp.logical_not(even))):

        @pl.when(case)
        def _(par=par):
            for n, block in enumerate(PACK[par]):
                packed[n] = rows[block]

    for n, (first, count) in enumerate(PARTS):
        stores.append(start(packed.at[pl.ds(first, count)], outs[1 + n], sems.at[9 + n]))
    for c in stores:
        c.wait()


def fill_band(size, stage, hi_ref, lo_ref, shift, rows):
    for a in rows:
        for c in range(6):
            e = c - a - shift
            at = (pl.ds(a * size, size), pl.ds(c * size, size))
            if 0 <= e < 4:
                hi_ref[at], lo_ref[at] = halves(stage[4 * a + e])
            else:
                hi_ref[at] = jnp.zeros((size, size), BF16)
                lo_ref[at] = jnp.zeros((size, size), BF16)


def gather_pair(even, packed, own, stage, sems, first):
    base = 8 if own else jnp.where(even, 16, 0)
    rotated = jnp.logical_not(even) if own else even
    places = ((base + jnp.where(rotated, 1, 0), 0, 7), (base + jnp.where(rotated, 0, 7), 7, 1))
    return [
        start(packed.at[pl.ds(n, count)], stage.at[pl.ds(at, count)], sems.at[first + k])
        for k, (at, n, count) in enumerate(places)
    ]


def gather_next(even, packed, stage, sem):
    return start(packed.at[pl.ds(0, 7)], stage.at[pl.ds(jnp.where(even, 1, 16), 7)], sem)


def product_own(size, where, u_any, p_mask_any, p_any, pe_z, pe_y, pc, pc_y, *refs):
    t_own, ud_hi, ud_lo, oth_hi, oth_lo, p_mask, p, stages, u, hi, lo, sems = refs
    even, layer = where[0] % 2 == 0, where[1]
    copies = [start(u_any, u, sems.at[0])]
    copies += [start(p_any, p, sems.at[1]), start(p_mask_any, p_mask, sems.at[2])]
    copies += gather_pair(even, pe_y, False, stages.at[0], sems, 3)
    copies += gather_pair(even, pc, True, stages.at[1], sems, 5)
    copies += gather_pair(even, pc_y, False, stages.at[1], sems, 7)
    copies += [gather_next(even, pe_z, stages.at[0], sems.at[9])]
    ud_hi[...] = jnp.zeros_like(ud_hi)
    ud_lo[...] = jnp.zeros_like(ud_lo)
    for c in copies:
        c.wait()
    for i in range(4):
        cols = pl.ds(aligned(slot_base(i, layer), size), 4 * size)
        rows = pl.ds(i * size, size)
        ud_hi[rows, cols], ud_lo[rows, cols] = joined([u[i, m] for m in range(4)], 1)
    for a in range(2):
        for e in range(4):
            stages[0, 8 + 4 * a + e] = p[a, 0, 2 * e] * p_mask[a, 0, 2 * e].astype(F32)
    fill_band(size, stages.at[0], hi, lo, -2, range(6))
    for i in range(4):
        cols = pl.ds(aligned(slot_base(i, layer), size), 4 * size)
        rows = pl.ds(i * size, size)
        t_own[i] = dot3((ud_hi[rows, cols], ud_lo[rows, cols]), (hi[cols, cols], lo[cols, cols]), 0)
    fill_band(size, stages.at[1], oth_hi, oth_lo, -1, (2, 3))
    for case, rows in ((even, (4, 5)), (jnp.logical_not(even), (0, 1))):

        @pl.when(case)
        def _(rows=rows):
            fill_band(size, stages.at[1], oth_hi, oth_lo, -1, rows)


def product_rows(total_rows, size, where, send, t_mask, t_own, others, hi, lo, t_hi, t_lo):
    slab, layer = where[0], where[1]
    for q in range(2):
        i = 2 * q + (1 - layer if send else layer)
        base = q + 1 - layer if send else q
        rows = pl.ds(aligned(q if send else q + layer, size), 4 * size)
        cols = pl.ds(aligned(q + 1 if send else q + layer, size), 4 * size)
        left = joined([others[i, m] for m in range(4)], 1)
        total = t_own[i] + dot3(left, (hi[rows, cols], lo[rows, cols]), 0)
        kept = []
        for m in range(4):
            col = slab * 4 + 2 * (base + m) - 4 + layer
            keep = jnp.where((col >= 0) & (col < total_rows), t_mask[i, m], 0).astype(F32)
            kept.append(total[:, m * size : (m + 1) * size] * keep)
        t_hi[q], t_lo[q] = joined(kept, 1)


def product_send(total_rows, size, where, t_mask_any, t_own, ud_hi, ud_lo, hi_in, lo_in, u_cross, pc_z, *refs):
    t_hi, t_lo, ss, hi, lo, t_mask, stage, u_oth, sems = refs
    even, layer = where[0] % 2 == 0, where[1]
    z_copy = gather_next(even, pc_z, stage, sems.at[1])
    x_copies = [start(u_cross.at[2 * q + 1 - layer], u_oth.at[2 * q + 1 - layer], sems.at[3 * q]) for q in range(2)]
    mask_copy = start(t_mask_any, t_mask, sems.at[2])
    z_copy.wait()
    for case, rows in ((even, (0, 1)), (jnp.logical_not(even), (4, 5))):

        @pl.when(case)
        def _(rows=rows):
            fill_band(size, stage, hi, lo, -1, rows)

    mask_copy.wait()
    for c in x_copies:
        c.wait()
    product_rows(total_rows, size, where, True, t_mask, t_own, u_oth, hi, lo, t_hi, t_lo)
    for q in range(2):
        cols = pl.ds(aligned(q + 1 - layer, size), 4 * size)
        sums = dot3((t_hi[q], t_lo[q]), (ud_hi[:, cols], ud_lo[:, cols]), 1)
        for r in range(4):
            ss[q, r] = sums[:, r * size : (r + 1) * size]


def product_keep(total_rows, size, where, t_mask_any, t_own, hi, lo, u_cross, t_hi, t_lo, t_mask, u_oth, sems):
    layer = where[1]
    copies = [start(u_cross.at[2 * q + layer], u_oth.at[2 * q + layer], sems.at[q]) for q in range(2)]
    copies.append(start(t_mask_any, t_mask, sems.at[2]))
    for c in copies:
        c.wait()
    product_rows(total_rows, size, where, False, t_mask, t_own, u_oth, hi, lo, t_hi, t_lo)


def gather_halo(u_y, u_z, stage, sems):
    spots = [stage.at[pl.ds(at, n)] for at, n in (*PARTS, (16, 7), (23, 5))]
    return [start(src, spot, sems.at[n]) for n, (src, spot) in enumerate(zip([*u_y, *u_z], spots))]


def fill_halo(size, where, stage, uh_hi, uh_lo, rows=(0, 1, 2, 3)):
    even, layer = where[0] % 2 == 0, where[1]
    uh_hi[...] = jnp.zeros_like(uh_hi)
    uh_lo[...] = jnp.zeros_like(uh_lo)
    for below_at, above_at, pack, case in ((16, 0, PACK[1], even), (0, 16, PACK[0], jnp.logical_not(even))):

        @pl.when(case)
        def _(below_at=below_at, above_at=above_at, pack=pack):
            for first, above in ((below_at, 0), (above_at, 1)):
                for n, (r, m) in enumerate(pack[: 16 if first == 0 else 12]):
                    if r not in rows or (above and r == 3):
                        continue
                    at = pl.ds((above * len(rows) + rows.index(r)) * size, size)
                    cols = pl.ds(aligned(slot_base(r, layer) + 4 * above + m, size), size)
                    uh_hi[at, cols], uh_lo[at, cols] = halves(stage[first + n])


def halo_sums(size, i, base, t_rows, uh_hi, uh_lo, ts=(0, 1, 2, 3)):
    cols = pl.ds(aligned(base + 2, size), 4 * size)
    rows = [pl.ds(aligned(jnp.where(t < i, len(ts) + n, n), size), size) for n, t in enumerate(ts)]
    hi = jnp.concatenate([uh_hi[r, cols] for r in rows], axis=0)
    lo = jnp.concatenate([uh_lo[r, cols] for r in rows], axis=0)
    return dot3(t_rows, (hi, lo), 1)


def send_halo(size, ts, where, *refs):
    u_y, u_z, t_hi, t_lo = refs[0:2], refs[2:-7], refs[-7], refs[-6]
    out, stage, uh_hi, uh_lo, sems = refs[-5:]
    layer = where[1]
    for c in gather_halo(u_y, u_z, stage, sems):
        c.wait()
    fill_halo(size, where, stage, uh_hi, uh_lo, ts)
    for q in range(2):
        sums = halo_sums(size, 2 * q + 1 - layer, q + 1 - layer, (t_hi[q], t_lo[q]), uh_hi, uh_lo, ts)
        for n in range(len(ts)):
            out[q, n] = sums[:, n * size : (n + 1) * size]


def out_keep(total_rows, where, o_mask, q, o):
    col = where[0] * 4 + 2 * q + where[1] - 4 + o
    return jnp.where((col >= 0) & (col < total_rows), o_mask[q, 0, o], 0).astype(F32)


def keep_rows(total_rows, size, where, o_mask, ss, halo, *refs):
    u_y, u_z, t_hi, t_lo, ud_hi, ud_lo = refs[0:2], refs[2:4], *refs[4:8]
    out_any, part, out, stage, uh_hi, uh_lo, sems = refs[8:]
    for c in gather_halo(u_y, u_z, stage, sems):
        c.wait()
    fill_halo(size, where, stage, uh_hi, uh_lo)
    stores = []
    for q in range(2):
        i = 2 * q + where[1]
        sums = halo_sums(size, i, q, (t_hi[q], t_lo[q]), uh_hi, uh_lo)
        for t in range(4):
            o = (8 - i + t) % 8
            keep = out_keep(total_rows, where, o_mask, q, o)
            value = sums[:, t * size : (t + 1) * size]
            if t < 2:
                out[q, 4 + t] = (value + halo[q, t]) * keep
                stores.append(start(out.at[q, 4 + t], out_any.at[q, 0, o], sems.at[4 + 2 * q + t]))
            else:
                part[q, t - 2] = value * keep
        cols = pl.ds(q * size, 4 * size)
        sums = dot3((t_hi[q], t_lo[q]), (ud_hi[:, cols], ud_lo[:, cols]), 1)
        for r in range(4):
            o = (4 - i + r) % 8
            keep = out_keep(total_rows, where, o_mask, q, o)
            out[q, r] = (sums[:, r * size : (r + 1) * size] + ss[q, r]) * keep
            stores.append(start(out.at[q, r], out_any.at[q, 0, o], sems.at[8 + 4 * q + r]))
    for c in stores:
        c.wait()


def combine(total_rows, where, o_mask, part, halo, kept_any, out_any, done, sems):
    stores = []
    for q in range(2):
        for t in range(2):
            o = (10 - 2 * q - where[1] + t) % 8
            done[q, t] = part[q, t] + halo[q, t] * out_keep(total_rows, where, o_mask, q, o)
            stores.append(start(done.at[q, t], out_any.at[q, 0, o], sems.at[2 * q + t]))
    for s in stores:
        s.wait()


def after(x, *others):
    return lax.optimization_barrier((x, *others))[0]


def on_device(u_values, u_mask, p_values, p_mask, t_mask, out_mask):
    size = u_values.shape[-1]
    slabs = lax.axis_size(SLABS)
    total_rows = slabs * u_values.shape[0]
    swap = [(0, 1), (1, 0)]
    pair = [(s, s ^ 1) for s in range(slabs)]
    onward = [(s, s + 2) for s in range(0, slabs - 2, 2)] + [(s, s - 2) for s in range(3, slabs, 2)]

    def over_layer(x):
        return lax.ppermute(x, "layer", swap)

    def over_pair(x):
        return lax.ppermute(x, SLABS, pair)

    def onto(x):
        return lax.ppermute(x, SLABS, onward)

    def sems(n):
        return pltpu.SemaphoreType.DMA((n,))

    eight = shape(2, 4, size, size)
    wide = 6 * size
    unit = 3 * 2 * (4 * size) ** 2 * size
    po, pe = call(
        keep_p,
        [vmem(8, size, size)] * 2,
        [HBM, HBM],
        [pltpu.SMEM(p_mask.shape, jnp.int32), vmem(*p_values.shape), sems(3)],
    )(p_mask, p_values)
    pc = over_layer(po)
    pe_y = over_pair(pe)
    u_mask, t_mask = u_mask[:, :, 0], t_mask[:, :, 0]
    u_own, *packed = call(
        keep_u,
        [shape(4, 4, size, size)] + [shape(n, size, size) for _, n in PARTS],
        [HBM, HBM],
        [pltpu.SMEM(u_mask.shape, jnp.int32), vmem(*u_values.shape), vmem(4, 4, size, size)]
        + [vmem(16, size, size), sems(11)],
    )(u_mask, u_values)
    u_oth = over_layer(after(u_own, pc))
    pe_z = onto(after(pe_y[:7], u_own))
    pc_y = over_pair(pc)
    pc_z = onto(pc_y)
    t_like = (4, size, 4 * size)
    band = [vmem(wide, wide, dtype=BF16)] * 2
    own_rows = [vmem(4 * size, wide, dtype=BF16)] * 2
    t_own, ud_hi, ud_lo, *oth = call(
        functools.partial(product_own, size),
        [vmem(*t_like), *own_rows, *band],
        [HBM, HBM, HBM, ANY] + [HBM] * 3,
        [pltpu.SMEM(p_mask.shape, jnp.int32), vmem(*p_values.shape)]
        + [vmem(2, 24, size, size), vmem(4, 4, size, size), *band, sems(10)],
        flops=4 * unit,
    )(u_own, p_mask, p_values, pe_z, pe_y, pc, pc_y)
    u_y = [over_pair(after(x, pc)) for x in packed]
    u_z = [onto(after(u_y[0], t_own))]
    t_mask = after(t_mask, u_y[0])
    rows = [vmem(2, size, 4 * size, dtype=BF16)] * 2
    masks = pltpu.SMEM(t_mask.shape, jnp.int32)
    *t_send, ss, hi, lo = call(
        functools.partial(product_send, total_rows, size),
        [*rows, vmem(2, 4, size, size), *band],
        [HBM] + [VMEM] * 5 + [ANY] * 2,
        [masks, vmem(24, size, size), vmem(4, 4, size, size), sems(4)],
        flops=4 * unit,
        alias={4: 3, 5: 4},
    )(t_mask, t_own, ud_hi, ud_lo, *oth, u_oth, pc_z)
    ss_got = over_layer(ss)
    t_keep = call(
        functools.partial(product_keep, total_rows, size),
        rows,
        [HBM] + [VMEM] * 3 + [ANY],
        [masks, vmem(4, 4, size, size), sems(3)],
        flops=2 * unit,
    )(t_mask, t_own, hi, lo, u_oth)
    u_z.append(onto(after(u_y[1][:5], t_send[0])))
    halos = []
    halo_scratch = [vmem(28, size, size)] + [vmem(4 * size, 9 * size, dtype=BF16)] * 2 + [sems(4)]
    for ts in ((0, 1), (2, 3)):
        nz = 1 if ts[0] == 0 else 2
        (halo,) = call(
            functools.partial(send_halo, size, ts),
            [vmem(2, 2, size, size)],
            [HBM] * 2 + [ANY] * nz + [VMEM] * 2,
            halo_scratch,
            flops=unit,
        )(*u_y, *u_z[:nz], t_send[0], after(t_send[1], *halos))
        halos.append(halo)
    halos = [over_layer(x) for x in halos]
    kept, part = call(
        functools.partial(keep_rows, total_rows, size),
        [shape(*p_values.shape), vmem(2, 2, size, size)],
        [SMEM] + [VMEM] * 2 + [HBM] * 2 + [ANY] * 2 + [VMEM] * 4,
        [vmem(2, 6, size, size), vmem(28, size, size)] + [vmem(8 * size, 9 * size, dtype=BF16)] * 2 + [sems(16)],
        flops=40 * unit,
    )(out_mask, ss_got, halos[0], *u_y, *u_z, *t_keep, ud_hi, ud_lo)
    (out,) = call(
        functools.partial(combine, total_rows),
        [shape(*p_values.shape)],
        [SMEM, VMEM, VMEM, ANY],
        [vmem(2, 2, size, size), sems(4)],
        alias={3: 0},
        limit=16,
    )(out_mask, part, halos[1], kept)
    return out


def solution(mesh):
    placed = (
        P(SLABS, None, "layer", None, None),
        P(SLABS, None, "layer"),
        P(SLABS, "layer", None, None, None),
        P(SLABS, "layer", None),
        P(SLABS, None, "layer"),
        P(SLABS, "layer", None),
    )
    return jax.shard_map(
        on_device,
        mesh=mesh,
        in_specs=placed,
        out_specs=P(SLABS, "layer", None, None, None),
        check_vma=False,
    )
```

```python
import functools

import jax
import jax.numpy as jnp
from jax import lax
from jax.experimental import pallas as pl
from jax.experimental.pallas import tpu as pltpu
from jax.sharding import PartitionSpec as P

SLABS = ("row", "col")
F32 = jnp.float32
BF16 = jnp.bfloat16
VMEM = pl.BlockSpec(memory_space=pltpu.VMEM)
SMEM = pl.BlockSpec(memory_space=pltpu.SMEM)
ANY = pl.BlockSpec(memory_space=pl.ANY)
HBM = object()

PACK = (
    [(0, 0), (0, 1), (0, 2), (0, 3), (1, 0), (1, 1), (1, 2), (1, 3), (2, 0), (2, 1), (2, 2), (2, 3)]
    + [(3, 0), (3, 1), (3, 2), (3, 3)],
    [(0, 2), (0, 3), (1, 1), (1, 2), (1, 3), (2, 1), (2, 2), (2, 3), (3, 0), (3, 1), (3, 2), (3, 3)]
    + [(0, 0), (0, 1), (1, 0), (2, 0)],
)
PARTS = ((0, 7), (7, 9))


def shape(*dims, dtype=F32):
    return jax.ShapeDtypeStruct(dims, dtype)


def vmem(*dims, dtype=F32):
    return pltpu.VMEM(dims, dtype)


def call(body, outs, ins, scratch=(), flops=0, alias=None, limit=24):
    def kernel(*refs):
        slab = lax.axis_index("row") * lax.axis_size("col") + lax.axis_index("col")
        body((slab, lax.axis_index("layer")), *refs)

    def run(*args):
        placed = [pltpu.with_memory_space_constraint(x, pltpu.HBM) if spec is HBM else x for spec, x in zip(ins, args)]
        return pl.pallas_call(
            kernel,
            out_shape=outs,
            in_specs=[ANY if spec is HBM else spec for spec in ins],
            out_specs=[ANY if isinstance(x, jax.ShapeDtypeStruct) else VMEM for x in outs],
            scratch_shapes=list(scratch),
            input_output_aliases=alias or {},
            cost_estimate=pl.CostEstimate(flops=flops, bytes_accessed=0, transcendentals=0),
            compiler_params=pltpu.CompilerParams(vmem_limit_bytes=limit << 20),
        )(*placed)

    return run


def halves(x):
    high = x.astype(BF16)
    return high, (x - high.astype(F32)).astype(BF16)


def dot3(a, b, rhs_contract):
    one = functools.partial(
        lax.dot_general,
        dimension_numbers=(((1,), (rhs_contract,)), ((), ())),
        preferred_element_type=F32,
    )
    return one(a[0], b[0]) + (one(a[0], b[1]) + one(a[1], b[0]))


def joined(blocks, axis):
    return [jnp.concatenate(x, axis=axis) for x in zip(*[halves(b) for b in blocks])]


def aligned(block, size):
    return pl.multiple_of(block * size, size)


def slot_base(i, layer):
    return i // 2 if i % 2 == 0 else (i + 1) // 2 - layer


def start(src, dst, sem):
    copy = pltpu.make_async_copy(src, dst, sem)
    copy.start()
    return copy


def keep_p(where, p_mask_any, p_any, *refs):
    outs, (p_mask, p, sems) = refs[0:2], refs[2:]
    even = where[0] % 2 == 0
    copies = [start(p_any.at[a], p.at[a], sems.at[a]) for a in range(2)]
    start(p_mask_any, p_mask, sems.at[2]).wait()
    for a in range(2):
        copies[a].wait()
        for o in range(8):
            n = 4 * a + o // 2
            outs[1 - o % 2][jnp.where(even, n, (n + 7) % 8)] = p[a, 0, o] * p_mask[a, 0, o].astype(F32)


def keep_u(where, u_mask_any, u_any, *refs):
    outs, (u_mask, u, rows, packed, sems) = refs[0:3], refs[3:]
    copies = [start(u_any.at[i], u.at[i], sems.at[i]) for i in range(4)]
    start(u_mask_any, u_mask, sems.at[4]).wait()
    even = where[0] % 2 == 0
    stores = []
    for i in range(4):
        copies[i].wait()
        for m in range(4):
            rows[i, m] = u[i, m, 0] * u_mask[i, m].astype(F32)
        stores.append(start(rows.at[i], outs[0].at[i], sems.at[5 + i]))
    for par, case in ((0, even), (1, jnp.logical_not(even))):

        @pl.when(case)
        def _(par=par):
            for n, block in enumerate(PACK[par]):
                packed[n] = rows[block]

    for n, (first, count) in enumerate(PARTS):
        stores.append(start(packed.at[pl.ds(first, count)], outs[1 + n], sems.at[9 + n]))
    for c in stores:
        c.wait()


def fill_band(size, stage, hi_ref, lo_ref, shift, rows):
    for a in rows:
        for c in range(6):
            e = c - a - shift
            at = (pl.ds(a * size, size), pl.ds(c * size, size))
            if 0 <= e < 4:
                hi_ref[at], lo_ref[at] = halves(stage[4 * a + e])
            else:
                hi_ref[at] = jnp.zeros((size, size), BF16)
                lo_ref[at] = jnp.zeros((size, size), BF16)


def gather_pair(even, packed, own, stage, sems, first):
    base = 8 if own else jnp.where(even, 16, 0)
    rotated = jnp.logical_not(even) if own else even
    places = ((base + jnp.where(rotated, 1, 0), 0, 7), (base + jnp.where(rotated, 0, 7), 7, 1))
    return [
        start(packed.at[pl.ds(n, count)], stage.at[pl.ds(at, count)], sems.at[first + k])
        for k, (at, n, count) in enumerate(places)
    ]


def gather_next(even, packed, stage, sem):
    return start(packed, stage.at[pl.ds(jnp.where(even, 1, 16), 7)], sem)


def product_own(size, where, u_any, p_mask_any, p_any, pe_z, pe_y, pc, pc_y, *refs):
    t_own, ud_hi, ud_lo, oth_hi, oth_lo, p_mask, p, stages, u, hi, lo, sems = refs
    even, layer = where[0] % 2 == 0, where[1]
    copies = [start(u_any, u, sems.at[0])]
    copies += [start(p_any, p, sems.at[1]), start(p_mask_any, p_mask, sems.at[2])]
    copies += gather_pair(even, pe_y, False, stages.at[0], sems, 3)
    copies += gather_pair(even, pc, True, stages.at[1], sems, 5)
    copies += gather_pair(even, pc_y, False, stages.at[1], sems, 7)
    copies += [gather_next(even, pe_z, stages.at[0], sems.at[9])]
    ud_hi[...] = jnp.zeros_like(ud_hi)
    ud_lo[...] = jnp.zeros_like(ud_lo)
    for c in copies:
        c.wait()
    for i in range(4):
        cols = pl.ds(aligned(slot_base(i, layer), size), 4 * size)
        rows = pl.ds(i * size, size)
        ud_hi[rows, cols], ud_lo[rows, cols] = joined([u[i, m] for m in range(4)], 1)
    for a in range(2):
        for e in range(4):
            stages[0, 8 + 4 * a + e] = p[a, 0, 2 * e] * p_mask[a, 0, 2 * e].astype(F32)
    fill_band(size, stages.at[0], hi, lo, -2, range(6))
    for i in range(4):
        cols = pl.ds(aligned(slot_base(i, layer), size), 4 * size)
        rows = pl.ds(i * size, size)
        t_own[i] = dot3((ud_hi[rows, cols], ud_lo[rows, cols]), (hi[cols, cols], lo[cols, cols]), 0)
    fill_band(size, stages.at[1], oth_hi, oth_lo, -1, (2, 3))
    for case, rows in ((even, (4, 5)), (jnp.logical_not(even), (0, 1))):

        @pl.when(case)
        def _(rows=rows):
            fill_band(size, stages.at[1], oth_hi, oth_lo, -1, rows)


def product_rows(total_rows, size, where, send, t_mask, t_own, others, hi, lo, t_hi, t_lo):
    slab, layer = where[0], where[1]
    for q in range(2):
        i = 2 * q + (1 - layer if send else layer)
        base = q + 1 - layer if send else q
        rows = pl.ds(aligned(q if send else q + layer, size), 4 * size)
        cols = pl.ds(aligned(q + 1 if send else q + layer, size), 4 * size)
        left = joined([others[i, m] for m in range(4)], 1)
        total = t_own[i] + dot3(left, (hi[rows, cols], lo[rows, cols]), 0)
        kept = []
        for m in range(4):
            col = slab * 4 + 2 * (base + m) - 4 + layer
            keep = jnp.where((col >= 0) & (col < total_rows), t_mask[i, m], 0).astype(F32)
            kept.append(total[:, m * size : (m + 1) * size] * keep)
        t_hi[q], t_lo[q] = joined(kept, 1)


def product_send(total_rows, size, where, t_mask_any, t_own, ud_hi, ud_lo, hi_in, lo_in, u_cross, pc_z, *refs):
    t_hi, t_lo, ss, hi, lo, t_mask, stage, u_oth, sems = refs
    even, layer = where[0] % 2 == 0, where[1]
    z_copy = gather_next(even, pc_z, stage, sems.at[1])
    x_copies = [start(u_cross.at[2 * q + 1 - layer], u_oth.at[2 * q + 1 - layer], sems.at[3 * q]) for q in range(2)]
    mask_copy = start(t_mask_any, t_mask, sems.at[2])
    z_copy.wait()
    for case, rows in ((even, (0, 1)), (jnp.logical_not(even), (4, 5))):

        @pl.when(case)
        def _(rows=rows):
            fill_band(size, stage, hi, lo, -1, rows)

    mask_copy.wait()
    for c in x_copies:
        c.wait()
    product_rows(total_rows, size, where, True, t_mask, t_own, u_oth, hi, lo, t_hi, t_lo)
    for q in range(2):
        cols = pl.ds(aligned(q + 1 - layer, size), 4 * size)
        sums = dot3((t_hi[q], t_lo[q]), (ud_hi[:, cols], ud_lo[:, cols]), 1)
        for r in range(4):
            ss[q, r] = sums[:, r * size : (r + 1) * size]


def product_keep(total_rows, size, where, t_mask_any, t_own, hi, lo, u_cross, t_hi, t_lo, t_mask, u_oth, sems):
    layer = where[1]
    copies = [start(u_cross.at[2 * q + layer], u_oth.at[2 * q + layer], sems.at[q]) for q in range(2)]
    copies.append(start(t_mask_any, t_mask, sems.at[2]))
    for c in copies:
        c.wait()
    product_rows(total_rows, size, where, False, t_mask, t_own, u_oth, hi, lo, t_hi, t_lo)


def gather_halo(u_y, u_z, stage, sems):
    spots = [stage.at[pl.ds(at, n)] for at, n in (*PARTS, (16, 7), (23, 5))]
    return [start(src, spot, sems.at[n]) for n, (src, spot) in enumerate(zip([*u_y, *u_z], spots))]


def fill_halo(size, where, stage, uh_hi, uh_lo, rows=(0, 1, 2, 3)):
    even, layer = where[0] % 2 == 0, where[1]
    uh_hi[...] = jnp.zeros_like(uh_hi)
    uh_lo[...] = jnp.zeros_like(uh_lo)
    for below_at, above_at, pack, case in ((16, 0, PACK[1], even), (0, 16, PACK[0], jnp.logical_not(even))):

        @pl.when(case)
        def _(below_at=below_at, above_at=above_at, pack=pack):
            for first, above in ((below_at, 0), (above_at, 1)):
                for n, (r, m) in enumerate(pack[: 16 if first == 0 else 12]):
                    if r not in rows or (above and r == 3):
                        continue
                    at = pl.ds((above * len(rows) + rows.index(r)) * size, size)
                    cols = pl.ds(aligned(slot_base(r, layer) + 4 * above + m, size), size)
                    uh_hi[at, cols], uh_lo[at, cols] = halves(stage[first + n])


def halo_sums(size, i, base, t_rows, uh_hi, uh_lo, ts=(0, 1, 2, 3)):
    cols = pl.ds(aligned(base + 2, size), 4 * size)
    rows = [pl.ds(aligned(jnp.where(t < i, len(ts) + n, n), size), size) for n, t in enumerate(ts)]
    hi = jnp.concatenate([uh_hi[r, cols] for r in rows], axis=0)
    lo = jnp.concatenate([uh_lo[r, cols] for r in rows], axis=0)
    return dot3(t_rows, (hi, lo), 1)


def send_halo(size, ts, where, *refs):
    u_y, u_z, t_hi, t_lo = refs[0:2], refs[2:-7], refs[-7], refs[-6]
    out, stage, uh_hi, uh_lo, sems = refs[-5:]
    layer = where[1]
    for c in gather_halo(u_y, u_z, stage, sems):
        c.wait()
    fill_halo(size, where, stage, uh_hi, uh_lo, ts)
    for q in range(2):
        sums = halo_sums(size, 2 * q + 1 - layer, q + 1 - layer, (t_hi[q], t_lo[q]), uh_hi, uh_lo, ts)
        for n in range(len(ts)):
            out[q, n] = sums[:, n * size : (n + 1) * size]


def out_keep(total_rows, where, o_mask, q, o):
    col = where[0] * 4 + 2 * q + where[1] - 4 + o
    return jnp.where((col >= 0) & (col < total_rows), o_mask[q, 0, o], 0).astype(F32)


def keep_rows(total_rows, size, where, o_mask, ss, halo, *refs):
    u_y, u_z, t_hi, t_lo, ud_hi, ud_lo = refs[0:2], refs[2:4], *refs[4:8]
    out_any, part, out, stage, uh_hi, uh_lo, sems = refs[8:]
    for c in gather_halo(u_y, u_z, stage, sems):
        c.wait()
    fill_halo(size, where, stage, uh_hi, uh_lo)
    stores = []
    for q in range(2):
        i = 2 * q + where[1]
        sums = halo_sums(size, i, q, (t_hi[q], t_lo[q]), uh_hi, uh_lo)
        for t in range(4):
            o = (8 - i + t) % 8
            keep = out_keep(total_rows, where, o_mask, q, o)
            value = sums[:, t * size : (t + 1) * size]
            if t < 2:
                out[q, 4 + t] = (value + halo[q, t]) * keep
                stores.append(start(out.at[q, 4 + t], out_any.at[q, 0, o], sems.at[4 + 2 * q + t]))
            else:
                part[q, t - 2] = value * keep
        cols = pl.ds(q * size, 4 * size)
        sums = dot3((t_hi[q], t_lo[q]), (ud_hi[:, cols], ud_lo[:, cols]), 1)
        for r in range(4):
            o = (4 - i + r) % 8
            keep = out_keep(total_rows, where, o_mask, q, o)
            out[q, r] = (sums[:, r * size : (r + 1) * size] + ss[q, r]) * keep
            stores.append(start(out.at[q, r], out_any.at[q, 0, o], sems.at[8 + 4 * q + r]))
    for c in stores:
        c.wait()


def combine(total_rows, where, o_mask, part, halo, kept_any, out_any, done, sems):
    stores = []
    for q in range(2):
        for t in range(2):
            o = (10 - 2 * q - where[1] + t) % 8
            done[q, t] = part[q, t] + halo[q, t] * out_keep(total_rows, where, o_mask, q, o)
            stores.append(start(done.at[q, t], out_any.at[q, 0, o], sems.at[2 * q + t]))
    for s in stores:
        s.wait()


def after(x, *others):
    return lax.optimization_barrier((x, *others))[0]


def on_device(u_values, u_mask, p_values, p_mask, t_mask, out_mask):
    size = u_values.shape[-1]
    slabs = lax.axis_size(SLABS)
    total_rows = slabs * u_values.shape[0]
    swap = [(0, 1), (1, 0)]
    pair = [(s, s ^ 1) for s in range(slabs)]
    onward = [(s, s + 2) for s in range(0, slabs - 2, 2)] + [(s, s - 2) for s in range(3, slabs, 2)]

    def over_layer(x):
        return lax.ppermute(x, "layer", swap)

    def over_pair(x):
        return lax.ppermute(x, SLABS, pair)

    def onto(x):
        return lax.ppermute(x, SLABS, onward)

    def sems(n):
        return pltpu.SemaphoreType.DMA((n,))

    eight = shape(2, 4, size, size)
    wide = 6 * size
    unit = 3 * 2 * (4 * size) ** 2 * size
    po, pe = call(
        keep_p,
        [vmem(8, size, size)] * 2,
        [HBM, HBM],
        [pltpu.SMEM(p_mask.shape, jnp.int32), vmem(*p_values.shape), sems(3)],
    )(p_mask, p_values)
    pc = over_layer(po)
    pe_y = over_pair(pe)
    u_mask, t_mask = u_mask[:, :, 0], t_mask[:, :, 0]
    u_own, *packed = call(
        keep_u,
        [shape(4, 4, size, size)] + [shape(n, size, size) for _, n in PARTS],
        [HBM, HBM],
        [pltpu.SMEM(u_mask.shape, jnp.int32), vmem(*u_values.shape), vmem(4, 4, size, size)]
        + [vmem(16, size, size), sems(11)],
    )(u_mask, u_values)
    u_oth = over_layer(after(u_own, pc))
    pe_z = onto(after(pe_y[:7], u_own))
    pc_y = over_pair(after(pc, u_own))
    pc_z = onto(pc_y[:7])
    t_like = (4, size, 4 * size)
    band = [vmem(wide, wide, dtype=BF16)] * 2
    own_rows = [vmem(4 * size, wide, dtype=BF16)] * 2
    t_own, ud_hi, ud_lo, *oth = call(
        functools.partial(product_own, size),
        [vmem(*t_like), *own_rows, *band],
        [HBM, HBM, HBM, ANY] + [HBM] * 3,
        [pltpu.SMEM(p_mask.shape, jnp.int32), vmem(*p_values.shape)]
        + [vmem(2, 24, size, size), vmem(4, 4, size, size), *band, sems(10)],
        flops=40 * unit,
    )(u_own, p_mask, p_values, pe_z, pe_y, pc, pc_y)
    u_y = [over_pair(after(x, pc)) for x in packed]
    u_z = [onto(after(u_y[0], t_own))]
    t_mask = after(t_mask, u_y[0])
    rows = [vmem(2, size, 4 * size, dtype=BF16)] * 2
    masks = pltpu.SMEM(t_mask.shape, jnp.int32)
    *t_send, ss, hi, lo = call(
        functools.partial(product_send, total_rows, size),
        [*rows, vmem(2, 4, size, size), *band],
        [HBM] + [VMEM] * 5 + [ANY] * 2,
        [masks, vmem(24, size, size), vmem(4, 4, size, size), sems(4)],
        flops=4 * unit,
        alias={4: 3, 5: 4},
    )(t_mask, t_own, ud_hi, ud_lo, *oth, u_oth, pc_z)
    ss_got = over_layer(ss)
    t_keep = call(
        functools.partial(product_keep, total_rows, size),
        rows,
        [HBM] + [VMEM] * 3 + [ANY],
        [masks, vmem(4, 4, size, size), sems(3)],
        flops=2 * unit,
    )(t_mask, t_own, hi, lo, u_oth)
    u_z.append(onto(after(u_y[1][:5], t_send[0])))
    halos = []
    halo_scratch = [vmem(28, size, size)] + [vmem(4 * size, 9 * size, dtype=BF16)] * 2 + [sems(4)]
    for ts in ((0, 1), (2, 3)):
        nz = 1 if ts[0] == 0 else 2
        (halo,) = call(
            functools.partial(send_halo, size, ts),
            [vmem(2, 2, size, size)],
            [HBM] * 2 + [ANY] * nz + [VMEM] * 2,
            halo_scratch,
            flops=unit,
        )(*u_y, *u_z[:nz], t_send[0], after(t_send[1], *halos))
        halos.append(halo)
    halos = [over_layer(x) for x in halos]
    kept, part = call(
        functools.partial(keep_rows, total_rows, size),
        [shape(*p_values.shape), vmem(2, 2, size, size)],
        [SMEM] + [VMEM] * 2 + [HBM] * 2 + [ANY] * 2 + [VMEM] * 4,
        [vmem(2, 6, size, size), vmem(28, size, size)] + [vmem(8 * size, 9 * size, dtype=BF16)] * 2 + [sems(16)],
        flops=40 * unit,
    )(out_mask, ss_got, halos[0], *u_y, *u_z, *t_keep, ud_hi, ud_lo)
    (out,) = call(
        functools.partial(combine, total_rows),
        [shape(*p_values.shape)],
        [SMEM, VMEM, VMEM, ANY],
        [vmem(2, 2, size, size), sems(4)],
        alias={3: 0},
        limit=16,
    )(out_mask, part, halos[1], kept)
    return out


def solution(mesh):
    placed = (
        P(SLABS, None, "layer", None, None),
        P(SLABS, None, "layer"),
        P(SLABS, "layer", None, None, None),
        P(SLABS, "layer", None),
        P(SLABS, None, "layer"),
        P(SLABS, "layer", None),
    )
    return jax.shard_map(
        on_device,
        mesh=mesh,
        in_specs=placed,
        out_specs=P(SLABS, "layer", None, None, None),
        check_vma=False,
    )
```

```python
import functools

import jax
import jax.numpy as jnp
from jax import lax
from jax.experimental import pallas as pl
from jax.experimental.pallas import tpu as pltpu
from jax.sharding import PartitionSpec as P

SLABS = ("row", "col")
F32 = jnp.float32
BF16 = jnp.bfloat16
VMEM = pl.BlockSpec(memory_space=pltpu.VMEM)
SMEM = pl.BlockSpec(memory_space=pltpu.SMEM)
ANY = pl.BlockSpec(memory_space=pl.ANY)
HBM = object()

PACK = (
    [(0, 0), (0, 1), (0, 2), (0, 3), (1, 0), (1, 1), (1, 2), (1, 3), (2, 0), (2, 1), (2, 2), (2, 3)]
    + [(3, 0), (3, 1), (3, 2), (3, 3)],
    [(0, 2), (0, 3), (1, 1), (1, 2), (1, 3), (2, 1), (2, 2), (2, 3), (3, 0), (3, 1), (3, 2), (3, 3)]
    + [(0, 0), (0, 1), (1, 0), (2, 0)],
)
PARTS = ((0, 7), (7, 9))


def shape(*dims, dtype=F32):
    return jax.ShapeDtypeStruct(dims, dtype)


def vmem(*dims, dtype=F32):
    return pltpu.VMEM(dims, dtype)


def call(body, outs, ins, scratch=(), flops=0, alias=None, limit=24):
    def kernel(*refs):
        slab = lax.axis_index("row") * lax.axis_size("col") + lax.axis_index("col")
        body((slab, lax.axis_index("layer")), *refs)

    def run(*args):
        placed = [pltpu.with_memory_space_constraint(x, pltpu.HBM) if spec is HBM else x for spec, x in zip(ins, args)]
        return pl.pallas_call(
            kernel,
            out_shape=outs,
            in_specs=[ANY if spec is HBM else spec for spec in ins],
            out_specs=[ANY if isinstance(x, jax.ShapeDtypeStruct) else VMEM for x in outs],
            scratch_shapes=list(scratch),
            input_output_aliases=alias or {},
            cost_estimate=pl.CostEstimate(flops=flops, bytes_accessed=0, transcendentals=0),
            compiler_params=pltpu.CompilerParams(vmem_limit_bytes=limit << 20),
        )(*placed)

    return run


def halves(x):
    high = x.astype(BF16)
    return high, (x - high.astype(F32)).astype(BF16)


def dot3(a, b, rhs_contract):
    one = functools.partial(
        lax.dot_general,
        dimension_numbers=(((1,), (rhs_contract,)), ((), ())),
        preferred_element_type=F32,
    )
    return one(a[0], b[0]) + (one(a[0], b[1]) + one(a[1], b[0]))


def joined(blocks, axis):
    return [jnp.concatenate(x, axis=axis) for x in zip(*[halves(b) for b in blocks])]


def aligned(block, size):
    return pl.multiple_of(block * size, size)


def slot_base(i, layer):
    return i // 2 if i % 2 == 0 else (i + 1) // 2 - layer


def start(src, dst, sem):
    copy = pltpu.make_async_copy(src, dst, sem)
    copy.start()
    return copy


def keep_p(where, p_mask_any, p_any, *refs):
    outs, (p_mask, p, sems) = refs[0:2], refs[2:]
    even = where[0] % 2 == 0
    copies = [start(p_any.at[a], p.at[a], sems.at[a]) for a in range(2)]
    start(p_mask_any, p_mask, sems.at[2]).wait()
    for a in range(2):
        copies[a].wait()
        for o in range(8):
            n = 4 * a + o // 2
            outs[1 - o % 2][jnp.where(even, n, (n + 7) % 8)] = p[a, 0, o] * p_mask[a, 0, o].astype(F32)


def keep_u(where, u_mask_any, u_any, *refs):
    outs, (u_mask, u, rows, packed, sems) = refs[0:3], refs[3:]
    copies = [start(u_any.at[i], u.at[i], sems.at[i]) for i in range(4)]
    start(u_mask_any, u_mask, sems.at[4]).wait()
    even = where[0] % 2 == 0
    stores = []
    for i in range(4):
        copies[i].wait()
        for m in range(4):
            rows[i, m] = u[i, m, 0] * u_mask[i, m].astype(F32)
        stores.append(start(rows.at[i], outs[0].at[i], sems.at[5 + i]))
    for par, case in ((0, even), (1, jnp.logical_not(even))):

        @pl.when(case)
        def _(par=par):
            for n, block in enumerate(PACK[par]):
                packed[n] = rows[block]

    for n, (first, count) in enumerate(PARTS):
        stores.append(start(packed.at[pl.ds(first, count)], outs[1 + n], sems.at[9 + n]))
    for c in stores:
        c.wait()


def fill_band(size, stage, hi_ref, lo_ref, shift, rows, first=0):
    for a in rows:
        for c in range(6):
            e = c - a - shift
            at = (pl.ds(a * size, size), pl.ds(c * size, size))
            if 0 <= e < 4:
                hi_ref[at], lo_ref[at] = halves(stage[4 * a + e - first])
            else:
                hi_ref[at] = jnp.zeros((size, size), BF16)
                lo_ref[at] = jnp.zeros((size, size), BF16)


def gather_pair(even, packed, own, stage, sems, first):
    base = 8 if own else jnp.where(even, 16, 0)
    rotated = jnp.logical_not(even) if own else even
    places = ((base + jnp.where(rotated, 1, 0), 0, 7), (base + jnp.where(rotated, 0, 7), 7, 1))
    return [
        start(packed.at[pl.ds(n, count)], stage.at[pl.ds(at, count)], sems.at[first + k])
        for k, (at, n, count) in enumerate(places)
    ]


def gather_next(even, packed, stage, sem):
    return start(packed, stage.at[pl.ds(jnp.where(even, 1, 16), 7)], sem)


def product_own(size, where, u_any, p_mask_any, p_any, pe_z, pe_y, pc, pc_y, *refs):
    t_own, ud_hi, ud_lo, oth_hi, oth_lo, p_mask, p, stages, u, hi, lo, sems = refs
    even, layer = where[0] % 2 == 0, where[1]
    copies = [start(u_any, u, sems.at[0])]
    copies += [start(p_any, p, sems.at[1]), start(p_mask_any, p_mask, sems.at[2])]
    copies += gather_pair(even, pe_y, False, stages.at[0], sems, 3)
    copies += gather_pair(even, pc, True, stages.at[1], sems, 5)
    copies += gather_pair(even, pc_y, False, stages.at[1], sems, 7)
    copies += [gather_next(even, pe_z, stages.at[0], sems.at[9])]
    ud_hi[...] = jnp.zeros_like(ud_hi)
    ud_lo[...] = jnp.zeros_like(ud_lo)
    for c in copies:
        c.wait()
    for i in range(4):
        cols = pl.ds(aligned(slot_base(i, layer), size), 4 * size)
        rows = pl.ds(i * size, size)
        ud_hi[rows, cols], ud_lo[rows, cols] = joined([u[i, m] for m in range(4)], 1)
    for a in range(2):
        for e in range(4):
            stages[0, 8 + 4 * a + e] = p[a, 0, 2 * e] * p_mask[a, 0, 2 * e].astype(F32)
    fill_band(size, stages.at[0], hi, lo, -2, range(6))
    for i in range(4):
        cols = pl.ds(aligned(slot_base(i, layer), size), 4 * size)
        rows = pl.ds(i * size, size)
        t_own[i] = dot3((ud_hi[rows, cols], ud_lo[rows, cols]), (hi[cols, cols], lo[cols, cols]), 0)
    fill_band(size, stages.at[1], oth_hi, oth_lo, -1, (2, 3))
    for case, rows in ((even, (4, 5)), (jnp.logical_not(even), (0, 1))):

        @pl.when(case)
        def _(rows=rows):
            fill_band(size, stages.at[1], oth_hi, oth_lo, -1, rows)


def product_rows(total_rows, size, where, send, t_mask, t_own, others, hi, lo, t_hi, t_lo):
    slab, layer = where[0], where[1]
    for q in range(2):
        i = 2 * q + (1 - layer if send else layer)
        base = q + 1 - layer if send else q
        rows = pl.ds(aligned(q if send else q + layer, size), 4 * size)
        cols = pl.ds(aligned(q + 1 if send else q + layer, size), 4 * size)
        left = joined([others[i, m] for m in range(4)], 1)
        total = t_own[i] + dot3(left, (hi[rows, cols], lo[rows, cols]), 0)
        kept = []
        for m in range(4):
            col = slab * 4 + 2 * (base + m) - 4 + layer
            keep = jnp.where((col >= 0) & (col < total_rows), t_mask[i, m], 0).astype(F32)
            kept.append(total[:, m * size : (m + 1) * size] * keep)
        t_hi[q], t_lo[q] = joined(kept, 1)


def product_send(total_rows, size, where, t_mask_any, t_own, ud_hi, ud_lo, hi_in, lo_in, u_cross, pc_z, *refs):
    t_hi, t_lo, ss, hi, lo, t_mask, sem = refs
    even, layer = where[0] % 2 == 0, where[1]
    mask_copy = start(t_mask_any, t_mask, sem)
    for case, rows, first in ((even, (0, 1), 1), (jnp.logical_not(even), (4, 5), 16)):

        @pl.when(case)
        def _(rows=rows, first=first):
            fill_band(size, pc_z, hi, lo, -1, rows, first)

    mask_copy.wait()
    product_rows(total_rows, size, where, True, t_mask, t_own, u_cross, hi, lo, t_hi, t_lo)
    for q in range(2):
        cols = pl.ds(aligned(q + 1 - layer, size), 4 * size)
        sums = dot3((t_hi[q], t_lo[q]), (ud_hi[:, cols], ud_lo[:, cols]), 1)
        for r in range(4):
            ss[q, r] = sums[:, r * size : (r + 1) * size]


def product_keep(total_rows, size, where, t_mask_any, t_own, hi, lo, u_cross, t_hi, t_lo, t_mask, sem):
    start(t_mask_any, t_mask, sem).wait()
    product_rows(total_rows, size, where, False, t_mask, t_own, u_cross, hi, lo, t_hi, t_lo)


def gather_halo(pieces, stage, sems):
    spots = [stage.at[pl.ds(at, n)] for at, n in (*PARTS, (16, 7), (23, 5))]
    return [start(x, spot, sems.at[n]) for n, (x, spot) in enumerate(zip(pieces, spots)) if x is not None]


def fill_halo(size, where, stage, uh_hi, uh_lo, rows, blocks):
    even, layer = where[0] % 2 == 0, where[1]
    for below_at, above_at, pack, case in ((16, 0, PACK[1], even), (0, 16, PACK[0], jnp.logical_not(even))):

        @pl.when(case)
        def _(below_at=below_at, above_at=above_at, pack=pack):
            for first, above in ((below_at, 0), (above_at, 1)):
                for n, (r, m) in enumerate(pack):
                    if first + n not in blocks or r not in rows or (above and r == 3):
                        continue
                    at = pl.ds((above * len(rows) + rows.index(r)) * size, size)
                    cols = pl.ds(aligned(slot_base(r, layer) + 4 * above + m, size), size)
                    uh_hi[at, cols], uh_lo[at, cols] = halves(stage[first + n])


def halo_sums(size, i, base, t_rows, uh_hi, uh_lo, ts=(0, 1, 2, 3)):
    cols = pl.ds(aligned(base + 2, size), 4 * size)
    rows = [pl.ds(aligned(jnp.where(t < i, len(ts) + n, n), size), size) for n, t in enumerate(ts)]
    hi = jnp.concatenate([uh_hi[r, cols] for r in rows], axis=0)
    lo = jnp.concatenate([uh_lo[r, cols] for r in rows], axis=0)
    return dot3(t_rows, (hi, lo), 1)


def send_sums(size, ts, where, t_hi, t_lo, uh_hi, uh_lo, out):
    for q in range(2):
        i, base = 2 * q + 1 - where[1], q + 1 - where[1]
        sums = halo_sums(size, i, base, (t_hi[q], t_lo[q]), uh_hi, uh_lo, ts)
        for n in range(len(ts)):
            out[q, n] = sums[:, n * size : (n + 1) * size]


def first_halo(size, where, y0, y1, z0, t_hi, t_lo, out, uh_hi, uh_lo, stage, sems):
    copies = gather_halo((y0, y1, z0), stage, sems)
    uh_hi[...] = jnp.zeros_like(uh_hi)
    uh_lo[...] = jnp.zeros_like(uh_lo)
    for c in copies:
        c.wait()
    fill_halo(size, where, stage, uh_hi, uh_lo, (0, 1), range(23))
    send_sums(size, (0, 1), where, t_hi, t_lo, uh_hi, uh_lo, out)


def halo_matrix(size, where, y0, y1, z0, uh_hi, uh_lo, stage, sems):
    copies = gather_halo((y0, y1, z0), stage, sems)
    uh_hi[...] = jnp.zeros_like(uh_hi)
    uh_lo[...] = jnp.zeros_like(uh_lo)
    for c in copies:
        c.wait()
    fill_halo(size, where, stage, uh_hi, uh_lo, (2, 3), range(23))


def last_halo(size, where, z1, t_hi, t_lo, hi_in, lo_in, out, uh_hi, uh_lo, stage, sems):
    for c in gather_halo((None, None, None, z1), stage, sems):
        c.wait()
    fill_halo(size, where, stage, uh_hi, uh_lo, (2, 3), range(23, 28))
    send_sums(size, (2, 3), where, t_hi, t_lo, uh_hi, uh_lo, out)


def out_keep(total_rows, where, o_mask, q, o):
    col = where[0] * 4 + 2 * q + where[1] - 4 + o
    return jnp.where((col >= 0) & (col < total_rows), o_mask[q, 0, o], 0).astype(F32)


def keep_rows(total_rows, size, where, o_mask, ss, halo, *refs):
    (t_hi, t_lo), (ud_hi, ud_lo), first, last = (refs[2 * n : 2 * n + 2] for n in range(4))
    out_any, part, out, sems = refs[8:]
    stores = []
    for q in range(2):
        i = 2 * q + where[1]
        t_rows = (t_hi[q], t_lo[q])
        cols = pl.ds(q * size, 4 * size)
        own = dot3(t_rows, (ud_hi[:, cols], ud_lo[:, cols]), 1)
        near = halo_sums(size, i, q, t_rows, *first, (0, 1))
        for n in range(6):
            o = (4 - i + n) % 8
            keep = out_keep(total_rows, where, o_mask, q, o)
            if n < 4:
                out[q, n] = (own[:, n * size : (n + 1) * size] + ss[q, n]) * keep
            else:
                out[q, n] = (near[:, (n - 4) * size : (n - 3) * size] + halo[q, n - 4]) * keep
            stores.append(start(out.at[q, n], out_any.at[q, 0, o], sems.at[6 * q + n]))
        sums = halo_sums(size, i, q, t_rows, *last, (2, 3))
        for n in range(2):
            keep = out_keep(total_rows, where, o_mask, q, (10 - i + n) % 8)
            part[q, n] = sums[:, n * size : (n + 1) * size] * keep
    for c in stores:
        c.wait()


def combine(total_rows, where, o_mask, part, halo, kept_any, out_any, done, sems):
    stores = []
    for q in range(2):
        for t in range(2):
            o = (10 - 2 * q - where[1] + t) % 8
            done[q, t] = part[q, t] + halo[q, t] * out_keep(total_rows, where, o_mask, q, o)
            stores.append(start(done.at[q, t], out_any.at[q, 0, o], sems.at[2 * q + t]))
    for s in stores:
        s.wait()


def after(x, *others):
    return lax.optimization_barrier((x, *others))[0]


def on_device(u_values, u_mask, p_values, p_mask, t_mask, out_mask):
    size = u_values.shape[-1]
    slabs = lax.axis_size(SLABS)
    total_rows = slabs * u_values.shape[0]
    swap = [(0, 1), (1, 0)]
    pair = [(s, s ^ 1) for s in range(slabs)]
    onward = [(s, s + 2) for s in range(0, slabs - 2, 2)] + [(s, s - 2) for s in range(3, slabs, 2)]

    def over_layer(x):
        return lax.ppermute(x, "layer", swap)

    def over_pair(x):
        return lax.ppermute(x, SLABS, pair)

    def onto(x):
        return lax.ppermute(x, SLABS, onward)

    def sems(n):
        return pltpu.SemaphoreType.DMA((n,))

    eight = shape(2, 4, size, size)
    wide = 6 * size
    unit = 3 * 2 * (4 * size) ** 2 * size
    po, pe = call(
        keep_p,
        [vmem(8, size, size)] * 2,
        [HBM, HBM],
        [pltpu.SMEM(p_mask.shape, jnp.int32), vmem(*p_values.shape), sems(3)],
    )(p_mask, p_values)
    pc = over_layer(po)
    pe_y = over_pair(pe)
    u_mask, t_mask = u_mask[:, :, 0], t_mask[:, :, 0]
    u_own, *packed = call(
        keep_u,
        [shape(4, 4, size, size)] + [shape(n, size, size) for _, n in PARTS],
        [HBM, HBM],
        [pltpu.SMEM(u_mask.shape, jnp.int32), vmem(*u_values.shape), vmem(4, 4, size, size)]
        + [vmem(16, size, size), sems(11)],
    )(u_mask, u_values)
    u_oth = over_layer(after(u_own, pc))
    pe_z = onto(after(pe_y[:7], u_own))
    pc_y = over_pair(after(pc, u_own))
    pc_z = onto(pc_y[:7])
    t_like = (4, size, 4 * size)
    band = [vmem(wide, wide, dtype=BF16)] * 2
    own_rows = [vmem(4 * size, wide, dtype=BF16)] * 2
    t_own, ud_hi, ud_lo, *oth = call(
        functools.partial(product_own, size),
        [vmem(*t_like), *own_rows, *band],
        [HBM, HBM, HBM, ANY] + [HBM] * 3,
        [pltpu.SMEM(p_mask.shape, jnp.int32), vmem(*p_values.shape)]
        + [vmem(2, 24, size, size), vmem(4, 4, size, size), *band, sems(10)],
        flops=40 * unit,
    )(u_own, p_mask, p_values, pe_z, pe_y, pc, pc_y)
    u_y = [over_pair(after(x, pc)) for x in packed]
    u_z = [onto(after(u_y[0], t_own))]
    t_mask = after(t_mask, u_y[0])
    rows = [vmem(2, size, 4 * size, dtype=BF16)] * 2
    masks = pltpu.SMEM(t_mask.shape, jnp.int32)
    *t_send, ss, hi, lo = call(
        functools.partial(product_send, total_rows, size),
        [*rows, vmem(2, 4, size, size), *band],
        [HBM] + [VMEM] * 7,
        [masks, pltpu.SemaphoreType.DMA],
        flops=4 * unit,
        alias={4: 3, 5: 4},
    )(t_mask, t_own, ud_hi, ud_lo, *oth, u_oth, pc_z)
    ss_got = over_layer(ss)
    t_keep = call(
        functools.partial(product_keep, total_rows, size),
        rows,
        [HBM] + [VMEM] * 4,
        [masks, pltpu.SemaphoreType.DMA],
        flops=2 * unit,
    )(t_mask, t_own, hi, lo, u_oth)
    u_z.append(onto(after(u_y[1][:5], t_send[0])))
    uh = [vmem(4 * size, 9 * size, dtype=BF16)] * 2
    pair_sums = vmem(2, 2, size, size)
    stage = vmem(28, size, size)
    halo, *uh_first = call(
        functools.partial(first_halo, size),
        [pair_sums, *uh],
        [HBM, HBM, ANY, VMEM, VMEM],
        [stage, sems(3)],
        flops=unit,
    )(*u_y, u_z[0], *t_send)
    halo_got = over_layer(halo)
    uh_last = call(functools.partial(halo_matrix, size), uh, [HBM, HBM, ANY], [stage, sems(3)])(
        after(u_y[0], halo), u_y[1], u_z[0]
    )
    last, *uh_last = call(
        functools.partial(last_halo, size),
        [pair_sums, *uh],
        [ANY] + [VMEM] * 4,
        [stage, sems(4)],
        flops=unit,
        alias={3: 1, 4: 2},
    )(u_z[1], *t_send, *uh_last)
    last_got = over_layer(last)
    kept, part = call(
        functools.partial(keep_rows, total_rows, size),
        [shape(*p_values.shape), pair_sums],
        [SMEM] + [VMEM] * 10,
        [vmem(2, 6, size, size), sems(12)],
        flops=40 * unit,
    )(out_mask, ss_got, halo_got, *t_keep, ud_hi, ud_lo, *uh_first, *uh_last)
    (out,) = call(
        functools.partial(combine, total_rows),
        [shape(*p_values.shape)],
        [SMEM, VMEM, VMEM, ANY],
        [vmem(2, 2, size, size), sems(4)],
        alias={3: 0},
        limit=16,
    )(out_mask, part, last_got, kept)
    return out


def solution(mesh):
    placed = (
        P(SLABS, None, "layer", None, None),
        P(SLABS, None, "layer"),
        P(SLABS, "layer", None, None, None),
        P(SLABS, "layer", None),
        P(SLABS, None, "layer"),
        P(SLABS, "layer", None),
    )
    return jax.shard_map(
        on_device,
        mesh=mesh,
        in_specs=placed,
        out_specs=P(SLABS, "layer", None, None, None),
        check_vma=False,
    )
```

```python
import functools

import jax
import jax.numpy as jnp
from jax import lax
from jax.experimental import pallas as pl
from jax.experimental.pallas import tpu as pltpu
from jax.sharding import PartitionSpec as P

SLABS = ("row", "col")
F32 = jnp.float32
BF16 = jnp.bfloat16
VMEM = pl.BlockSpec(memory_space=pltpu.VMEM)
SMEM = pl.BlockSpec(memory_space=pltpu.SMEM)
ANY = pl.BlockSpec(memory_space=pl.ANY)
HBM = object()

PACK = (
    [(0, 0), (0, 1), (0, 2), (0, 3), (1, 0), (1, 1), (1, 2), (1, 3), (2, 0), (2, 1), (2, 2), (2, 3)]
    + [(3, 0), (3, 1), (3, 2), (3, 3)],
    [(0, 2), (0, 3), (1, 1), (1, 2), (1, 3), (2, 1), (2, 2), (2, 3), (3, 0), (3, 1), (3, 2), (3, 3)]
    + [(0, 0), (0, 1), (1, 0), (2, 0)],
)
PARTS = ((0, 7), (7, 9))


def shape(*dims, dtype=F32):
    return jax.ShapeDtypeStruct(dims, dtype)


def vmem(*dims, dtype=F32):
    return pltpu.VMEM(dims, dtype)


def call(body, outs, ins, scratch=(), flops=0, alias=None, limit=24):
    def kernel(*refs):
        slab = lax.axis_index("row") * lax.axis_size("col") + lax.axis_index("col")
        body((slab, lax.axis_index("layer")), *refs)

    def run(*args):
        placed = [pltpu.with_memory_space_constraint(x, pltpu.HBM) if spec is HBM else x for spec, x in zip(ins, args)]
        return pl.pallas_call(
            kernel,
            out_shape=outs,
            in_specs=[ANY if spec is HBM else spec for spec in ins],
            out_specs=[ANY if isinstance(x, jax.ShapeDtypeStruct) else VMEM for x in outs],
            scratch_shapes=list(scratch),
            input_output_aliases=alias or {},
            cost_estimate=pl.CostEstimate(flops=flops, bytes_accessed=0, transcendentals=0),
            compiler_params=pltpu.CompilerParams(vmem_limit_bytes=limit << 20),
        )(*placed)

    return run


def halves(x):
    high = x.astype(BF16)
    return high, (x - high.astype(F32)).astype(BF16)


def dot3(a, b, rhs_contract):
    one = functools.partial(
        lax.dot_general,
        dimension_numbers=(((1,), (rhs_contract,)), ((), ())),
        preferred_element_type=F32,
    )
    return one(a[0], b[0]) + (one(a[0], b[1]) + one(a[1], b[0]))


def joined(blocks, axis):
    return [jnp.concatenate(x, axis=axis) for x in zip(*[halves(b) for b in blocks])]


def aligned(block, size):
    return pl.multiple_of(block * size, size)


def slot_base(i, layer):
    return i // 2 if i % 2 == 0 else (i + 1) // 2 - layer


def start(src, dst, sem):
    copy = pltpu.make_async_copy(src, dst, sem)
    copy.start()
    return copy


def keep_p(where, p_mask_any, p_any, *refs):
    outs, (p_mask, p, sems) = refs[0:2], refs[2:]
    even = where[0] % 2 == 0
    copies = [start(p_any.at[a], p.at[a], sems.at[a]) for a in range(2)]
    start(p_mask_any, p_mask, sems.at[2]).wait()
    for a in range(2):
        copies[a].wait()
        for o in range(8):
            n = 4 * a + o // 2
            outs[1 - o % 2][jnp.where(even, n, (n + 7) % 8)] = p[a, 0, o] * p_mask[a, 0, o].astype(F32)


def keep_u(where, u_mask_any, u_any, *refs):
    outs, (u_mask, u, rows, packed, sems) = refs[0:3], refs[3:]
    copies = [start(u_any.at[i], u.at[i], sems.at[i]) for i in range(4)]
    start(u_mask_any, u_mask, sems.at[4]).wait()
    even = where[0] % 2 == 0
    stores = []
    for i in range(4):
        copies[i].wait()
        for m in range(4):
            rows[i, m] = u[i, m, 0] * u_mask[i, m].astype(F32)
        stores.append(start(rows.at[i], outs[0].at[i], sems.at[5 + i]))
    for par, case in ((0, even), (1, jnp.logical_not(even))):

        @pl.when(case)
        def _(par=par):
            for n, block in enumerate(PACK[par]):
                packed[n] = rows[block]

    for n, (first, count) in enumerate(PARTS):
        stores.append(start(packed.at[pl.ds(first, count)], outs[1 + n], sems.at[9 + n]))
    for c in stores:
        c.wait()


def fill_band(size, stage, hi_ref, lo_ref, shift, rows, first=0):
    for a in rows:
        for c in range(6):
            e = c - a - shift
            at = (pl.ds(a * size, size), pl.ds(c * size, size))
            if 0 <= e < 4:
                hi_ref[at], lo_ref[at] = halves(stage[4 * a + e - first])
            else:
                hi_ref[at] = jnp.zeros((size, size), BF16)
                lo_ref[at] = jnp.zeros((size, size), BF16)


def gather_pair(even, packed, own, stage, sems, first):
    base = 8 if own else jnp.where(even, 16, 0)
    rotated = jnp.logical_not(even) if own else even
    places = ((base + jnp.where(rotated, 1, 0), 0, 7), (base + jnp.where(rotated, 0, 7), 7, 1))
    return [
        start(packed.at[pl.ds(n, count)], stage.at[pl.ds(at, count)], sems.at[first + k])
        for k, (at, n, count) in enumerate(places)
    ]


def gather_next(even, packed, stage, sem):
    return start(packed, stage.at[pl.ds(jnp.where(even, 1, 16), 7)], sem)


def product_own(total_rows, size, where, u_any, p_mask_any, p_any, t_mask_any, pe_z, pe_y, pc, pc_y, *refs):
    t_own, ud_hi, ud_lo, oth_hi, oth_lo, keeps, p_mask, t_mask, p, stages, u, hi, lo, sems = refs
    slab, layer = where[0], where[1]
    even = slab % 2 == 0
    copies = [start(u_any, u, sems.at[0])]
    copies += [start(p_any, p, sems.at[1]), start(p_mask_any, p_mask, sems.at[2])]
    copies += [start(t_mask_any, t_mask, sems.at[10])]
    copies += gather_pair(even, pe_y, False, stages.at[0], sems, 3)
    copies += gather_pair(even, pc, True, stages.at[1], sems, 5)
    copies += gather_pair(even, pc_y, False, stages.at[1], sems, 7)
    copies += [gather_next(even, pe_z, stages.at[0], sems.at[9])]
    ud_hi[...] = jnp.zeros_like(ud_hi)
    ud_lo[...] = jnp.zeros_like(ud_lo)
    for c in copies:
        c.wait()
    for i in range(4):
        cols = pl.ds(aligned(slot_base(i, layer), size), 4 * size)
        rows = pl.ds(i * size, size)
        ud_hi[rows, cols], ud_lo[rows, cols] = joined([u[i, m] for m in range(4)], 1)
        for m in range(4):
            col = slab * 4 + 2 * (slot_base(i, layer) + m) - 4 + layer
            keep = jnp.where((col >= 0) & (col < total_rows), t_mask[i, m], 0).astype(F32)
            keeps[i, m] = jnp.full(keeps.shape[2:], keep, F32)
    for a in range(2):
        for e in range(4):
            stages[0, 8 + 4 * a + e] = p[a, 0, 2 * e] * p_mask[a, 0, 2 * e].astype(F32)
    fill_band(size, stages.at[0], hi, lo, -2, range(6))
    for i in range(4):
        cols = pl.ds(aligned(slot_base(i, layer), size), 4 * size)
        rows = pl.ds(i * size, size)
        t_own[i] = dot3((ud_hi[rows, cols], ud_lo[rows, cols]), (hi[cols, cols], lo[cols, cols]), 0)
    fill_band(size, stages.at[1], oth_hi, oth_lo, -1, (2, 3))
    for case, rows in ((even, (4, 5)), (jnp.logical_not(even), (0, 1))):

        @pl.when(case)
        def _(rows=rows):
            fill_band(size, stages.at[1], oth_hi, oth_lo, -1, rows)


def product_rows(size, where, send, keeps, t_own, others, hi, lo, t_hi, t_lo):
    layer = where[1]
    for q in range(2):
        i = 2 * q + (1 - layer if send else layer)
        rows = pl.ds(aligned(q if send else q + layer, size), 4 * size)
        cols = pl.ds(aligned(q + 1 if send else q + layer, size), 4 * size)
        left = joined([others[i, m] for m in range(4)], 1)
        total = t_own[i] + dot3(left, (hi[rows, cols], lo[rows, cols]), 0)
        kept = [total[:, m * size : (m + 1) * size] * keeps[i, m, 0:1] for m in range(4)]
        t_hi[q], t_lo[q] = joined(kept, 1)


def product_send(size, where, keeps, t_own, ud_hi, ud_lo, hi_in, lo_in, u_cross, pc_z, t_hi, t_lo, ss, hi, lo):
    even, layer = where[0] % 2 == 0, where[1]
    for case, rows, first in ((even, (0, 1), 1), (jnp.logical_not(even), (4, 5), 16)):

        @pl.when(case)
        def _(rows=rows, first=first):
            fill_band(size, pc_z, hi, lo, -1, rows, first)

    product_rows(size, where, True, keeps, t_own, u_cross, hi, lo, t_hi, t_lo)
    for q in range(2):
        cols = pl.ds(aligned(q + 1 - layer, size), 4 * size)
        sums = dot3((t_hi[q], t_lo[q]), (ud_hi[:, cols], ud_lo[:, cols]), 1)
        for r in range(4):
            ss[q, r] = sums[:, r * size : (r + 1) * size]


def product_keep(size, where, keeps, t_own, hi, lo, u_cross, t_hi, t_lo):
    product_rows(size, where, False, keeps, t_own, u_cross, hi, lo, t_hi, t_lo)


def gather_halo(pieces, stage, sems):
    spots = [stage.at[pl.ds(at, n)] for at, n in (*PARTS, (16, 7), (23, 5))]
    return [start(x, spot, sems.at[n]) for n, (x, spot) in enumerate(zip(pieces, spots)) if x is not None]


def fill_halo(size, where, stage, uh_hi, uh_lo, rows, blocks):
    even, layer = where[0] % 2 == 0, where[1]
    for below_at, above_at, pack, case in ((16, 0, PACK[1], even), (0, 16, PACK[0], jnp.logical_not(even))):

        @pl.when(case)
        def _(below_at=below_at, above_at=above_at, pack=pack):
            for first, above in ((below_at, 0), (above_at, 1)):
                for n, (r, m) in enumerate(pack):
                    if first + n not in blocks or r not in rows or (above and r == 3):
                        continue
                    at = pl.ds((above * len(rows) + rows.index(r)) * size, size)
                    cols = pl.ds(aligned(slot_base(r, layer) + 4 * above + m, size), size)
                    uh_hi[at, cols], uh_lo[at, cols] = halves(stage[first + n])


def halo_sums(size, i, base, t_rows, uh_hi, uh_lo, ts=(0, 1, 2, 3)):
    cols = pl.ds(aligned(base + 2, size), 4 * size)
    rows = [pl.ds(aligned(jnp.where(t < i, len(ts) + n, n), size), size) for n, t in enumerate(ts)]
    hi = jnp.concatenate([uh_hi[r, cols] for r in rows], axis=0)
    lo = jnp.concatenate([uh_lo[r, cols] for r in rows], axis=0)
    return dot3(t_rows, (hi, lo), 1)


def send_sums(size, ts, where, t_hi, t_lo, uh_hi, uh_lo, out):
    for q in range(2):
        i, base = 2 * q + 1 - where[1], q + 1 - where[1]
        sums = halo_sums(size, i, base, (t_hi[q], t_lo[q]), uh_hi, uh_lo, ts)
        for n in range(len(ts)):
            out[q, n] = sums[:, n * size : (n + 1) * size]


def first_halo(size, where, y0, y1, z0, t_hi, t_lo, out, uh_hi, uh_lo, stage, sems):
    copies = gather_halo((y0, y1, z0), stage, sems)
    uh_hi[...] = jnp.zeros_like(uh_hi)
    uh_lo[...] = jnp.zeros_like(uh_lo)
    for c in copies:
        c.wait()
    fill_halo(size, where, stage, uh_hi, uh_lo, (0, 1), range(23))
    send_sums(size, (0, 1), where, t_hi, t_lo, uh_hi, uh_lo, out)


def halo_matrix(size, where, y0, y1, z0, uh_hi, uh_lo, stage, sems):
    copies = gather_halo((y0, y1, z0), stage, sems)
    uh_hi[...] = jnp.zeros_like(uh_hi)
    uh_lo[...] = jnp.zeros_like(uh_lo)
    for c in copies:
        c.wait()
    fill_halo(size, where, stage, uh_hi, uh_lo, (2, 3), range(23))


def last_halo(size, where, z1, t_hi, t_lo, hi_in, lo_in, out, uh_hi, uh_lo, stage, sems):
    for c in gather_halo((None, None, None, z1), stage, sems):
        c.wait()
    fill_halo(size, where, stage, uh_hi, uh_lo, (2, 3), range(23, 28))
    send_sums(size, (2, 3), where, t_hi, t_lo, uh_hi, uh_lo, out)


def out_keep(total_rows, where, o_mask, q, o):
    col = where[0] * 4 + 2 * q + where[1] - 4 + o
    return jnp.where((col >= 0) & (col < total_rows), o_mask[q, 0, o], 0).astype(F32)


def keep_rows(total_rows, size, where, o_mask, ss, halo, *refs):
    (t_hi, t_lo), (ud_hi, ud_lo), first, last = (refs[2 * n : 2 * n + 2] for n in range(4))
    out_any, part, keeps, out, sems = refs[8:]
    stores = []
    for q in range(2):
        i = 2 * q + where[1]
        t_rows = (t_hi[q], t_lo[q])
        cols = pl.ds(q * size, 4 * size)
        own = dot3(t_rows, (ud_hi[:, cols], ud_lo[:, cols]), 1)
        near = halo_sums(size, i, q, t_rows, *first, (0, 1))
        for n in range(6):
            o = (4 - i + n) % 8
            keep = out_keep(total_rows, where, o_mask, q, o)
            if n < 4:
                out[q, n] = (own[:, n * size : (n + 1) * size] + ss[q, n]) * keep
            else:
                out[q, n] = (near[:, (n - 4) * size : (n - 3) * size] + halo[q, n - 4]) * keep
            stores.append(start(out.at[q, n], out_any.at[q, 0, o], sems.at[6 * q + n]))
        sums = halo_sums(size, i, q, t_rows, *last, (2, 3))
        for n in range(2):
            keep = out_keep(total_rows, where, o_mask, q, (10 - i + n) % 8)
            part[q, n] = sums[:, n * size : (n + 1) * size] * keep
            keeps[q, n] = jnp.full(keeps.shape[2:], keep, F32)
    for c in stores:
        c.wait()


def combine(where, keeps, part, halo, kept_any, out_any, out, sems):
    stores = []
    for q in range(2):
        for n in range(2):
            o = (10 - 2 * q - where[1] + n) % 8
            out[q, n] = part[q, n] + halo[q, n] * keeps[q, n, 0:1]
            stores.append(start(out.at[q, n], out_any.at[q, 0, o], sems.at[2 * q + n]))
    for c in stores:
        c.wait()


def after(x, *others):
    return lax.optimization_barrier((x, *others))[0]


def on_device(u_values, u_mask, p_values, p_mask, t_mask, out_mask):
    size = u_values.shape[-1]
    slabs = lax.axis_size(SLABS)
    total_rows = slabs * u_values.shape[0]
    swap = [(0, 1), (1, 0)]
    pair = [(s, s ^ 1) for s in range(slabs)]
    onward = [(s, s + 2) for s in range(0, slabs - 2, 2)] + [(s, s - 2) for s in range(3, slabs, 2)]

    def over_layer(x):
        return lax.ppermute(x, "layer", swap)

    def over_pair(x):
        return lax.ppermute(x, SLABS, pair)

    def onto(x):
        return lax.ppermute(x, SLABS, onward)

    def sems(n):
        return pltpu.SemaphoreType.DMA((n,))

    eight = shape(2, 4, size, size)
    wide = 6 * size
    unit = 3 * 2 * (4 * size) ** 2 * size
    po, pe = call(
        keep_p,
        [vmem(8, size, size)] * 2,
        [HBM, HBM],
        [pltpu.SMEM(p_mask.shape, jnp.int32), vmem(*p_values.shape), sems(3)],
    )(p_mask, p_values)
    pc = over_layer(po)
    pe_y = over_pair(pe)
    u_mask, t_mask = u_mask[:, :, 0], t_mask[:, :, 0]
    u_own, *packed = call(
        keep_u,
        [shape(4, 4, size, size)] + [shape(n, size, size) for _, n in PARTS],
        [HBM, HBM],
        [pltpu.SMEM(u_mask.shape, jnp.int32), vmem(*u_values.shape), vmem(4, 4, size, size)]
        + [vmem(16, size, size), sems(11)],
    )(u_mask, u_values)
    u_oth = over_layer(after(u_own, pc))
    pe_z = onto(after(pe_y[:7], u_own))
    pc_y = over_pair(after(pc, u_own))
    pc_z = onto(pc_y[:7])
    t_like = (4, size, 4 * size)
    band = [vmem(wide, wide, dtype=BF16)] * 2
    own_rows = [vmem(4 * size, wide, dtype=BF16)] * 2
    t_own, ud_hi, ud_lo, *oth, keeps = call(
        functools.partial(product_own, total_rows, size),
        [vmem(*t_like), *own_rows, *band, vmem(4, 4, 8, size)],
        [HBM, HBM, HBM, HBM, ANY] + [HBM] * 3,
        [pltpu.SMEM(x.shape, jnp.int32) for x in (p_mask, t_mask)]
        + [vmem(*p_values.shape)]
        + [vmem(2, 24, size, size), vmem(4, 4, size, size), *band, sems(11)],
        flops=40 * unit,
    )(u_own, p_mask, p_values, t_mask, pe_z, pe_y, pc, pc_y)
    u_y = [over_pair(after(x, pc)) for x in packed]
    u_z = [onto(after(u_y[0], t_own))]
    keeps = after(keeps, u_y[0])
    rows = [vmem(2, size, 4 * size, dtype=BF16)] * 2
    *t_send, ss, hi, lo = call(
        functools.partial(product_send, size),
        [*rows, vmem(2, 4, size, size), *band],
        [VMEM] * 8,
        flops=4 * unit,
        alias={4: 3, 5: 4},
    )(keeps, t_own, ud_hi, ud_lo, *oth, u_oth, pc_z)
    ss_got = over_layer(ss)
    t_keep = call(
        functools.partial(product_keep, size),
        rows,
        [VMEM] * 5,
        flops=2 * unit,
    )(keeps, t_own, hi, lo, u_oth)
    u_z.append(onto(after(u_y[1][:5], t_send[0])))
    uh = [vmem(4 * size, 9 * size, dtype=BF16)] * 2
    pair_sums = vmem(2, 2, size, size)
    stage = vmem(28, size, size)
    halo, *uh_first = call(
        functools.partial(first_halo, size),
        [pair_sums, *uh],
        [HBM, HBM, ANY, VMEM, VMEM],
        [stage, sems(3)],
        flops=unit,
    )(*u_y, u_z[0], *t_send)
    halo_got = over_layer(halo)
    uh_last = call(functools.partial(halo_matrix, size), uh, [HBM, HBM, ANY], [stage, sems(3)])(
        after(u_y[0], halo), u_y[1], u_z[0]
    )
    last, *uh_last = call(
        functools.partial(last_halo, size),
        [pair_sums, *uh],
        [ANY] + [VMEM] * 4,
        [stage, sems(4)],
        flops=unit,
        alias={3: 1, 4: 2},
    )(u_z[1], *t_send, *uh_last)
    last_got = over_layer(last)
    kept, part, keeps = call(
        functools.partial(keep_rows, total_rows, size),
        [shape(*p_values.shape), pair_sums, vmem(2, 2, 8, size)],
        [SMEM] + [VMEM] * 10,
        [vmem(2, 6, size, size), sems(12)],
        flops=40 * unit,
    )(out_mask, ss_got, halo_got, *t_keep, ud_hi, ud_lo, *uh_first, *uh_last)
    (out,) = call(
        combine,
        [shape(*p_values.shape)],
        [VMEM, VMEM, VMEM, ANY],
        [vmem(2, 2, size, size), sems(4)],
        alias={3: 0},
        limit=16,
    )(keeps, part, last_got, kept)
    return out


def solution(mesh):
    placed = (
        P(SLABS, None, "layer", None, None),
        P(SLABS, None, "layer"),
        P(SLABS, "layer", None, None, None),
        P(SLABS, "layer", None),
        P(SLABS, None, "layer"),
        P(SLABS, "layer", None),
    )
    return jax.shard_map(
        on_device,
        mesh=mesh,
        in_specs=placed,
        out_specs=P(SLABS, "layer", None, None, None),
        check_vma=False,
    )
```

```python
import functools

import jax
import jax.numpy as jnp
from jax import lax
from jax.experimental import pallas as pl
from jax.experimental.pallas import tpu as pltpu
from jax.sharding import PartitionSpec as P

SLABS = ("row", "col")
F32 = jnp.float32
BF16 = jnp.bfloat16
VMEM = pl.BlockSpec(memory_space=pltpu.VMEM)
SMEM = pl.BlockSpec(memory_space=pltpu.SMEM)
ANY = pl.BlockSpec(memory_space=pl.ANY)
HBM = object()

PACK = (
    [(0, 0), (0, 1), (0, 2), (0, 3), (1, 0), (1, 1), (1, 2), (1, 3), (2, 0), (2, 1), (2, 2), (2, 3)]
    + [(3, 0), (3, 1), (3, 2), (3, 3)],
    [(0, 2), (0, 3), (1, 1), (1, 2), (1, 3), (2, 1), (2, 2), (2, 3), (3, 0), (3, 1), (3, 2), (3, 3)]
    + [(0, 0), (0, 1), (1, 0), (2, 0)],
)
PARTS = ((0, 7), (7, 9))


def shape(*dims, dtype=F32):
    return jax.ShapeDtypeStruct(dims, dtype)


def vmem(*dims, dtype=F32):
    return pltpu.VMEM(dims, dtype)


def call(body, outs, ins, scratch=(), flops=0, alias=None, limit=24):
    def kernel(*refs):
        slab = lax.axis_index("row") * lax.axis_size("col") + lax.axis_index("col")
        body((slab, lax.axis_index("layer")), *refs)

    def run(*args):
        placed = [pltpu.with_memory_space_constraint(x, pltpu.HBM) if spec is HBM else x for spec, x in zip(ins, args)]
        return pl.pallas_call(
            kernel,
            out_shape=outs,
            in_specs=[ANY if spec is HBM else spec for spec in ins],
            out_specs=[ANY if isinstance(x, jax.ShapeDtypeStruct) else VMEM for x in outs],
            scratch_shapes=list(scratch),
            input_output_aliases=alias or {},
            cost_estimate=pl.CostEstimate(flops=flops, bytes_accessed=0, transcendentals=0),
            compiler_params=pltpu.CompilerParams(vmem_limit_bytes=limit << 20),
        )(*placed)

    return run


def halves(x):
    high = x.astype(BF16)
    return high, (x - high.astype(F32)).astype(BF16)


def dot3(a, b, rhs_contract):
    one = functools.partial(
        lax.dot_general,
        dimension_numbers=(((1,), (rhs_contract,)), ((), ())),
        preferred_element_type=F32,
    )
    return one(a[0], b[0]) + (one(a[0], b[1]) + one(a[1], b[0]))


def joined(blocks, axis):
    return [jnp.concatenate(x, axis=axis) for x in zip(*[halves(b) for b in blocks])]


def aligned(block, size):
    return pl.multiple_of(block * size, size)


def slot_base(i, layer):
    return i // 2 if i % 2 == 0 else (i + 1) // 2 - layer


def start(src, dst, sem):
    copy = pltpu.make_async_copy(src, dst, sem)
    copy.start()
    return copy


def keep_p(where, p_mask_any, p_any, *refs):
    outs, (p_mask, p, sems) = refs[0:2], refs[2:]
    even = where[0] % 2 == 0
    copies = [start(p_any.at[a], p.at[a], sems.at[a]) for a in range(2)]
    start(p_mask_any, p_mask, sems.at[2]).wait()
    for a in range(2):
        copies[a].wait()
        for o in range(8):
            n = 4 * a + o // 2
            outs[1 - o % 2][jnp.where(even, n, (n + 7) % 8)] = p[a, 0, o] * p_mask[a, 0, o].astype(F32)


def keep_u(where, u_mask_any, u_any, *refs):
    outs, (u_mask, u, rows, packed, sems) = refs[0:3], refs[3:]
    copies = [start(u_any.at[i], u.at[i], sems.at[i]) for i in range(4)]
    start(u_mask_any, u_mask, sems.at[4]).wait()
    even = where[0] % 2 == 0
    stores = []
    for i in range(4):
        copies[i].wait()
        for m in range(4):
            rows[i, m] = u[i, m, 0] * u_mask[i, m].astype(F32)
        stores.append(start(rows.at[i], outs[0].at[i], sems.at[5 + i]))
    for par, case in ((0, even), (1, jnp.logical_not(even))):

        @pl.when(case)
        def _(par=par):
            for n, block in enumerate(PACK[par]):
                packed[n] = rows[block]

    for n, (first, count) in enumerate(PARTS):
        stores.append(start(packed.at[pl.ds(first, count)], outs[1 + n], sems.at[9 + n]))
    for c in stores:
        c.wait()


def fill_band(size, stage, hi_ref, lo_ref, shift, rows, first=0):
    for a in rows:
        for c in range(6):
            e = c - a - shift
            at = (pl.ds(a * size, size), pl.ds(c * size, size))
            if 0 <= e < 4:
                hi_ref[at], lo_ref[at] = halves(stage[4 * a + e - first])
            else:
                hi_ref[at] = jnp.zeros((size, size), BF16)
                lo_ref[at] = jnp.zeros((size, size), BF16)


def gather_pair(even, packed, own, stage, sems, first):
    base = 8 if own else jnp.where(even, 16, 0)
    rotated = jnp.logical_not(even) if own else even
    places = ((base + jnp.where(rotated, 1, 0), 0, 7), (base + jnp.where(rotated, 0, 7), 7, 1))
    return [
        start(packed.at[pl.ds(n, count)], stage.at[pl.ds(at, count)], sems.at[first + k])
        for k, (at, n, count) in enumerate(places)
    ]


def gather_next(even, packed, stage, sem):
    return start(packed, stage.at[pl.ds(jnp.where(even, 1, 16), 7)], sem)


def product_own(total_rows, size, where, u_any, p_mask_any, p_any, t_mask_any, pe_z, pe_y, pc, pc_y, *refs):
    t_own, ud_hi, ud_lo, oth_hi, oth_lo, keeps, p_mask, t_mask, p, stages, u, hi, lo, sems = refs
    slab, layer = where[0], where[1]
    even = slab % 2 == 0
    copies = [start(u_any, u, sems.at[0])]
    copies += [start(p_any, p, sems.at[1]), start(p_mask_any, p_mask, sems.at[2])]
    copies += [start(t_mask_any, t_mask, sems.at[10])]
    copies += gather_pair(even, pe_y, False, stages.at[0], sems, 3)
    copies += gather_pair(even, pc, True, stages.at[1], sems, 5)
    copies += gather_pair(even, pc_y, False, stages.at[1], sems, 7)
    copies += [gather_next(even, pe_z, stages.at[0], sems.at[9])]
    ud_hi[...] = jnp.zeros_like(ud_hi)
    ud_lo[...] = jnp.zeros_like(ud_lo)
    for c in copies:
        c.wait()
    for i in range(4):
        cols = pl.ds(aligned(slot_base(i, layer), size), 4 * size)
        rows = pl.ds(i * size, size)
        ud_hi[rows, cols], ud_lo[rows, cols] = joined([u[i, m] for m in range(4)], 1)
        for m in range(4):
            col = slab * 4 + 2 * (slot_base(i, layer) + m) - 4 + layer
            keep = jnp.where((col >= 0) & (col < total_rows), t_mask[i, m], 0).astype(F32)
            keeps[i, m] = jnp.full(keeps.shape[2:], keep, F32)
    for a in range(2):
        for e in range(4):
            stages[0, 8 + 4 * a + e] = p[a, 0, 2 * e] * p_mask[a, 0, 2 * e].astype(F32)
    fill_band(size, stages.at[0], hi, lo, -2, range(6))
    for i in range(4):
        cols = pl.ds(aligned(slot_base(i, layer), size), 4 * size)
        rows = pl.ds(i * size, size)
        t_own[i] = dot3((ud_hi[rows, cols], ud_lo[rows, cols]), (hi[cols, cols], lo[cols, cols]), 0)
    fill_band(size, stages.at[1], oth_hi, oth_lo, -1, (2, 3))
    for case, rows in ((even, (4, 5)), (jnp.logical_not(even), (0, 1))):

        @pl.when(case)
        def _(rows=rows):
            fill_band(size, stages.at[1], oth_hi, oth_lo, -1, rows)


def product_rows(size, where, send, keeps, t_own, others, hi, lo, t_hi, t_lo):
    layer = where[1]
    for q in range(2):
        i = 2 * q + (1 - layer if send else layer)
        rows = pl.ds(aligned(q if send else q + layer, size), 4 * size)
        cols = pl.ds(aligned(q + 1 if send else q + layer, size), 4 * size)
        left = joined([others[i, m] for m in range(4)], 1)
        total = t_own[i] + dot3(left, (hi[rows, cols], lo[rows, cols]), 0)
        kept = [total[:, m * size : (m + 1) * size] * keeps[i, m, 0:1] for m in range(4)]
        t_hi[q], t_lo[q] = joined(kept, 1)


def product_send(size, where, keeps, t_own, ud_hi, ud_lo, hi_in, lo_in, u_cross, pc_z, t_hi, t_lo, ss, hi, lo):
    even, layer = where[0] % 2 == 0, where[1]
    for case, rows, first in ((even, (0, 1), 1), (jnp.logical_not(even), (4, 5), 16)):

        @pl.when(case)
        def _(rows=rows, first=first):
            fill_band(size, pc_z, hi, lo, -1, rows, first)

    product_rows(size, where, True, keeps, t_own, u_cross, hi, lo, t_hi, t_lo)
    for q in range(2):
        cols = pl.ds(aligned(q + 1 - layer, size), 4 * size)
        sums = dot3((t_hi[q], t_lo[q]), (ud_hi[:, cols], ud_lo[:, cols]), 1)
        for r in range(4):
            ss[q, r] = sums[:, r * size : (r + 1) * size]


def product_keep(size, where, keeps, t_own, hi, lo, u_cross, t_hi, t_lo):
    product_rows(size, where, False, keeps, t_own, u_cross, hi, lo, t_hi, t_lo)


def gather_halo(pieces, stage, sems):
    spots = [stage.at[pl.ds(at, n)] for at, n in (*PARTS, (16, 7), (23, 5))]
    return [start(x, spot, sems.at[n]) for n, (x, spot) in enumerate(zip(pieces, spots)) if x is not None]


def fill_halo(size, where, stage, uh_hi, uh_lo, rows, blocks):
    even, layer = where[0] % 2 == 0, where[1]
    for below_at, above_at, pack, case in ((16, 0, PACK[1], even), (0, 16, PACK[0], jnp.logical_not(even))):

        @pl.when(case)
        def _(below_at=below_at, above_at=above_at, pack=pack):
            for first, above in ((below_at, 0), (above_at, 1)):
                for n, (r, m) in enumerate(pack):
                    if first + n not in blocks or r not in rows or (above and r == 3):
                        continue
                    at = pl.ds((above * len(rows) + rows.index(r)) * size, size)
                    cols = pl.ds(aligned(slot_base(r, layer) + 4 * above + m, size), size)
                    uh_hi[at, cols], uh_lo[at, cols] = halves(stage[first + n])


def halo_sums(size, i, base, t_rows, uh_hi, uh_lo, ts=(0, 1, 2, 3)):
    cols = pl.ds(aligned(base + 2, size), 4 * size)
    rows = [pl.ds(aligned(jnp.where(t < i, len(ts) + n, n), size), size) for n, t in enumerate(ts)]
    hi = jnp.concatenate([uh_hi[r, cols] for r in rows], axis=0)
    lo = jnp.concatenate([uh_lo[r, cols] for r in rows], axis=0)
    return dot3(t_rows, (hi, lo), 1)


def send_sums(size, ts, where, t_hi, t_lo, uh_hi, uh_lo, out):
    for q in range(2):
        i, base = 2 * q + 1 - where[1], q + 1 - where[1]
        sums = halo_sums(size, i, base, (t_hi[q], t_lo[q]), uh_hi, uh_lo, ts)
        for n in range(len(ts)):
            out[q, n] = sums[:, n * size : (n + 1) * size]


def first_halo(size, where, y0, y1, z0, t_hi, t_lo, out, uh_hi, uh_lo, stage, sems):
    copies = gather_halo((y0, y1, z0), stage, sems)
    uh_hi[...] = jnp.zeros_like(uh_hi)
    uh_lo[...] = jnp.zeros_like(uh_lo)
    for c in copies:
        c.wait()
    fill_halo(size, where, stage, uh_hi, uh_lo, (0, 1), range(23))
    send_sums(size, (0, 1), where, t_hi, t_lo, uh_hi, uh_lo, out)


def halo_matrix(size, where, y0, y1, z0, uh_hi, uh_lo, stage, sems):
    copies = gather_halo((y0, y1, z0), stage, sems)
    uh_hi[...] = jnp.zeros_like(uh_hi)
    uh_lo[...] = jnp.zeros_like(uh_lo)
    for c in copies:
        c.wait()
    fill_halo(size, where, stage, uh_hi, uh_lo, (2, 3), range(23))


def last_halo(size, where, z1, t_hi, t_lo, hi_in, lo_in, out, uh_hi, uh_lo, stage, sems):
    for c in gather_halo((None, None, None, z1), stage, sems):
        c.wait()
    fill_halo(size, where, stage, uh_hi, uh_lo, (2, 3), range(23, 28))
    send_sums(size, (2, 3), where, t_hi, t_lo, uh_hi, uh_lo, out)


def out_keep(total_rows, where, o_mask, q, o):
    col = where[0] * 4 + 2 * q + where[1] - 4 + o
    return jnp.where((col >= 0) & (col < total_rows), o_mask[q, 0, o], 0).astype(F32)


def keep_rows(total_rows, size, where, o_mask, ss, halo, *refs):
    (t_hi, t_lo), (ud_hi, ud_lo), first, last = (refs[2 * n : 2 * n + 2] for n in range(4))
    out_any, part, keeps, out, sems = refs[8:]
    stores = []
    for q in range(2):
        i = 2 * q + where[1]
        t_rows = (t_hi[q], t_lo[q])
        cols = pl.ds(q * size, 4 * size)
        own = dot3(t_rows, (ud_hi[:, cols], ud_lo[:, cols]), 1)
        near = halo_sums(size, i, q, t_rows, *first, (0, 1))
        for n in range(6):
            o = (4 - i + n) % 8
            keep = out_keep(total_rows, where, o_mask, q, o)
            if n < 4:
                out[q, n] = (own[:, n * size : (n + 1) * size] + ss[q, n]) * keep
            else:
                out[q, n] = (near[:, (n - 4) * size : (n - 3) * size] + halo[q, n - 4]) * keep
            stores.append(start(out.at[q, n], out_any.at[q, 0, o], sems.at[6 * q + n]))
        sums = halo_sums(size, i, q, t_rows, *last, (2, 3))
        for n in range(2):
            keep = out_keep(total_rows, where, o_mask, q, (10 - i + n) % 8)
            part[q, n] = sums[:, n * size : (n + 1) * size] * keep
            keeps[q, n] = jnp.full(keeps.shape[2:], keep, F32)
    for c in stores:
        c.wait()


def combine(where, keeps, part, halo, kept_any, out_any, out, sems):
    stores = []
    for q in range(2):
        for n in range(2):
            o = (10 - 2 * q - where[1] + n) % 8
            out[q, n] = part[q, n] + halo[q, n] * keeps[q, n, 0:1]
            stores.append(start(out.at[q, n], out_any.at[q, 0, o], sems.at[2 * q + n]))
    for c in stores:
        c.wait()


def after(x, *others):
    return lax.optimization_barrier((x, *others))[0]


def on_device(u_values, u_mask, p_values, p_mask, t_mask, out_mask):
    size = u_values.shape[-1]
    slabs = lax.axis_size(SLABS)
    total_rows = slabs * u_values.shape[0]
    swap = [(0, 1), (1, 0)]
    pair = [(s, s ^ 1) for s in range(slabs)]
    onward = [(s, s + 2) for s in range(0, slabs - 2, 2)] + [(s, s - 2) for s in range(3, slabs, 2)]

    def over_layer(x):
        return lax.ppermute(x, "layer", swap)

    def over_pair(x):
        return lax.ppermute(x, SLABS, pair)

    def onto(x):
        return lax.ppermute(x, SLABS, onward)

    def sems(n):
        return pltpu.SemaphoreType.DMA((n,))

    eight = shape(2, 4, size, size)
    wide = 6 * size
    unit = 3 * 2 * (4 * size) ** 2 * size
    po, pe = call(
        keep_p,
        [vmem(8, size, size)] * 2,
        [HBM, HBM],
        [pltpu.SMEM(p_mask.shape, jnp.int32), vmem(*p_values.shape), sems(3)],
    )(p_mask, p_values)
    pc = over_layer(po)
    pe_y = over_pair(pe)
    u_mask, t_mask = u_mask[:, :, 0], t_mask[:, :, 0]
    u_own, *packed = call(
        keep_u,
        [shape(4, 4, size, size)] + [shape(n, size, size) for _, n in PARTS],
        [HBM, HBM],
        [pltpu.SMEM(u_mask.shape, jnp.int32), vmem(*u_values.shape), vmem(4, 4, size, size)]
        + [vmem(16, size, size), sems(11)],
    )(u_mask, u_values)
    u_oth = over_layer(after(u_own, pc))
    pe_z = onto(after(pe_y[:7], u_own))
    pc_y = over_pair(after(pc, u_own))
    pc_z = onto(pc_y[:7])
    t_like = (4, size, 4 * size)
    band = [vmem(wide, wide, dtype=BF16)] * 2
    own_rows = [vmem(4 * size, wide, dtype=BF16)] * 2
    t_own, ud_hi, ud_lo, *oth, keeps = call(
        functools.partial(product_own, total_rows, size),
        [vmem(*t_like), *own_rows, *band, vmem(4, 4, 8, size)],
        [HBM, HBM, HBM, HBM, ANY] + [HBM] * 3,
        [pltpu.SMEM(x.shape, jnp.int32) for x in (p_mask, t_mask)]
        + [vmem(*p_values.shape)]
        + [vmem(2, 24, size, size), vmem(4, 4, size, size), *band, sems(11)],
        flops=22 * unit,
    )(u_own, p_mask, p_values, t_mask, pe_z, pe_y, pc, pc_y)
    u_y = [over_pair(after(x, pc)) for x in packed]
    u_z = [onto(after(u_y[0], t_own))]
    rows = [vmem(2, size, 4 * size, dtype=BF16)] * 2
    *t_send, ss, hi, lo = call(
        functools.partial(product_send, size),
        [*rows, vmem(2, 4, size, size), *band],
        [VMEM] * 8,
        flops=4 * unit,
        alias={4: 3, 5: 4},
    )(keeps, t_own, ud_hi, ud_lo, *oth, u_oth, pc_z)
    ss_got = over_layer(ss)
    t_keep = call(
        functools.partial(product_keep, size),
        rows,
        [VMEM] * 5,
        flops=2 * unit,
    )(keeps, t_own, hi, lo, u_oth)
    u_z.append(onto(after(u_y[1][:5], t_send[0])))
    uh = [vmem(4 * size, 9 * size, dtype=BF16)] * 2
    pair_sums = vmem(2, 2, size, size)
    stage = vmem(28, size, size)
    halo, *uh_first = call(
        functools.partial(first_halo, size),
        [pair_sums, *uh],
        [HBM, HBM, ANY, VMEM, VMEM],
        [stage, sems(3)],
        flops=unit,
    )(*u_y, u_z[0], *t_send)
    halo_got = over_layer(halo)
    uh_last = call(functools.partial(halo_matrix, size), uh, [HBM, HBM, ANY], [stage, sems(3)])(
        after(u_y[0], halo), u_y[1], u_z[0]
    )
    last, *uh_last = call(
        functools.partial(last_halo, size),
        [pair_sums, *uh],
        [ANY] + [VMEM] * 4,
        [stage, sems(4)],
        flops=unit,
        alias={3: 1, 4: 2},
    )(u_z[1], *t_send, *uh_last)
    last_got = over_layer(last)
    kept, part, keeps = call(
        functools.partial(keep_rows, total_rows, size),
        [shape(*p_values.shape), pair_sums, vmem(2, 2, 8, size)],
        [SMEM] + [VMEM] * 10,
        [vmem(2, 6, size, size), sems(12)],
        flops=40 * unit,
    )(out_mask, ss_got, halo_got, *t_keep, ud_hi, ud_lo, *uh_first, *uh_last)
    (out,) = call(
        combine,
        [shape(*p_values.shape)],
        [VMEM, VMEM, VMEM, ANY],
        [vmem(2, 2, size, size), sems(4)],
        alias={3: 0},
        limit=16,
    )(keeps, part, last_got, kept)
    return out


def solution(mesh):
    placed = (
        P(SLABS, None, "layer", None, None),
        P(SLABS, None, "layer"),
        P(SLABS, "layer", None, None, None),
        P(SLABS, "layer", None),
        P(SLABS, None, "layer"),
        P(SLABS, "layer", None),
    )
    return jax.shard_map(
        on_device,
        mesh=mesh,
        in_specs=placed,
        out_specs=P(SLABS, "layer", None, None, None),
        check_vma=False,
    )
```

```python
import functools

import jax
import jax.numpy as jnp
from jax import lax
from jax.experimental import pallas as pl
from jax.experimental.pallas import tpu as pltpu
from jax.sharding import PartitionSpec as P

SLABS = ("row", "col")
F32 = jnp.float32
BF16 = jnp.bfloat16
VMEM = pl.BlockSpec(memory_space=pltpu.VMEM)
SMEM = pl.BlockSpec(memory_space=pltpu.SMEM)
ANY = pl.BlockSpec(memory_space=pl.ANY)
HBM = object()

PACK = (
    [(0, 0), (0, 1), (0, 2), (0, 3), (1, 0), (1, 1), (1, 2), (1, 3), (2, 0), (2, 1), (2, 2), (2, 3)]
    + [(3, 0), (3, 1), (3, 2), (3, 3)],
    [(0, 2), (0, 3), (1, 1), (1, 2), (1, 3), (2, 1), (2, 2), (2, 3), (3, 0), (3, 1), (3, 2), (3, 3)]
    + [(0, 0), (0, 1), (1, 0), (2, 0)],
)
PARTS = ((0, 7), (7, 9))


def shape(*dims, dtype=F32):
    return jax.ShapeDtypeStruct(dims, dtype)


def vmem(*dims, dtype=F32):
    return pltpu.VMEM(dims, dtype)


def call(body, outs, ins, scratch=(), flops=0, alias=None, limit=24):
    def kernel(*refs):
        slab = lax.axis_index("row") * lax.axis_size("col") + lax.axis_index("col")
        body((slab, lax.axis_index("layer")), *refs)

    def run(*args):
        placed = [pltpu.with_memory_space_constraint(x, pltpu.HBM) if spec is HBM else x for spec, x in zip(ins, args)]
        return pl.pallas_call(
            kernel,
            out_shape=outs,
            in_specs=[ANY if spec is HBM else spec for spec in ins],
            out_specs=[ANY if isinstance(x, jax.ShapeDtypeStruct) else VMEM for x in outs],
            scratch_shapes=list(scratch),
            input_output_aliases=alias or {},
            cost_estimate=pl.CostEstimate(flops=flops, bytes_accessed=0, transcendentals=0),
            compiler_params=pltpu.CompilerParams(vmem_limit_bytes=limit << 20),
        )(*placed)

    return run


def halves(x):
    high = x.astype(BF16)
    return high, (x - high.astype(F32)).astype(BF16)


def dot3(a, b, rhs_contract):
    one = functools.partial(
        lax.dot_general,
        dimension_numbers=(((1,), (rhs_contract,)), ((), ())),
        preferred_element_type=F32,
    )
    return one(a[0], b[0]) + (one(a[0], b[1]) + one(a[1], b[0]))


def joined(blocks, axis):
    return [jnp.concatenate(x, axis=axis) for x in zip(*[halves(b) for b in blocks])]


def aligned(block, size):
    return pl.multiple_of(block * size, size)


def slot_base(i, layer):
    return i // 2 if i % 2 == 0 else (i + 1) // 2 - layer


def start(src, dst, sem):
    copy = pltpu.make_async_copy(src, dst, sem)
    copy.start()
    return copy


def keep_p(where, p_mask_any, p_any, *refs):
    outs, (p_mask, p, sems) = refs[0:2], refs[2:]
    even = where[0] % 2 == 0
    copies = [start(p_any.at[a], p.at[a], sems.at[a]) for a in range(2)]
    start(p_mask_any, p_mask, sems.at[2]).wait()
    for a in range(2):
        copies[a].wait()
        for o in range(8):
            n = 4 * a + o // 2
            outs[1 - o % 2][jnp.where(even, n, (n + 7) % 8)] = p[a, 0, o] * p_mask[a, 0, o].astype(F32)


def keep_u(where, u_mask_any, u_any, *refs):
    outs, (u_mask, u, rows, packed, sems) = refs[0:3], refs[3:]
    copies = [start(u_any.at[i], u.at[i], sems.at[i]) for i in range(4)]
    start(u_mask_any, u_mask, sems.at[4]).wait()
    even = where[0] % 2 == 0
    stores = []
    for i in range(4):
        copies[i].wait()
        for m in range(4):
            rows[i, m] = u[i, m, 0] * u_mask[i, m].astype(F32)
        stores.append(start(rows.at[i], outs[0].at[i], sems.at[5 + i]))
    for par, case in ((0, even), (1, jnp.logical_not(even))):

        @pl.when(case)
        def _(par=par):
            for n, block in enumerate(PACK[par]):
                packed[n] = rows[block]

    for n, (first, count) in enumerate(PARTS):
        stores.append(start(packed.at[pl.ds(first, count)], outs[1 + n], sems.at[9 + n]))
    for c in stores:
        c.wait()


def fill_band(size, stage, hi_ref, lo_ref, shift, rows, first=0):
    for a in rows:
        for c in range(6):
            e = c - a - shift
            at = (pl.ds(a * size, size), pl.ds(c * size, size))
            if 0 <= e < 4:
                hi_ref[at], lo_ref[at] = halves(stage[4 * a + e - first])
            else:
                hi_ref[at] = jnp.zeros((size, size), BF16)
                lo_ref[at] = jnp.zeros((size, size), BF16)


def gather_pair(even, packed, own, stage, sems, first):
    base = 8 if own else jnp.where(even, 16, 0)
    rotated = jnp.logical_not(even) if own else even
    places = ((base + jnp.where(rotated, 1, 0), 0, 7), (base + jnp.where(rotated, 0, 7), 7, 1))
    return [
        start(packed.at[pl.ds(n, count)], stage.at[pl.ds(at, count)], sems.at[first + k])
        for k, (at, n, count) in enumerate(places)
    ]


def gather_next(even, packed, stage, sem):
    return start(packed, stage.at[pl.ds(jnp.where(even, 1, 16), 7)], sem)


def product_own(total_rows, size, where, u_any, p_mask_any, p_any, t_mask_any, pe_z, pe_y, pc, pc_y, *refs):
    t_own, ud_hi, ud_lo, oth_hi, oth_lo, keeps, p_mask, t_mask, p, stages, u, hi, lo, sems = refs
    slab, layer = where[0], where[1]
    even = slab % 2 == 0
    copies = [start(u_any, u, sems.at[0])]
    copies += [start(p_any, p, sems.at[1]), start(p_mask_any, p_mask, sems.at[2])]
    copies += [start(t_mask_any, t_mask, sems.at[10])]
    copies += gather_pair(even, pe_y, False, stages.at[0], sems, 3)
    copies += gather_pair(even, pc, True, stages.at[1], sems, 5)
    copies += gather_pair(even, pc_y, False, stages.at[1], sems, 7)
    copies += [gather_next(even, pe_z, stages.at[0], sems.at[9])]
    ud_hi[...] = jnp.zeros_like(ud_hi)
    ud_lo[...] = jnp.zeros_like(ud_lo)
    for c in copies:
        c.wait()
    for i in range(4):
        cols = pl.ds(aligned(slot_base(i, layer), size), 4 * size)
        rows = pl.ds(i * size, size)
        ud_hi[rows, cols], ud_lo[rows, cols] = joined([u[i, m] for m in range(4)], 1)
        for m in range(4):
            col = slab * 4 + 2 * (slot_base(i, layer) + m) - 4 + layer
            keep = jnp.where((col >= 0) & (col < total_rows), t_mask[i, m], 0).astype(F32)
            keeps[i, m] = jnp.full(keeps.shape[2:], keep, F32)
    for a in range(2):
        for e in range(4):
            stages[0, 8 + 4 * a + e] = p[a, 0, 2 * e] * p_mask[a, 0, 2 * e].astype(F32)
    fill_band(size, stages.at[0], hi, lo, -2, range(6))
    for i in range(4):
        cols = pl.ds(aligned(slot_base(i, layer), size), 4 * size)
        rows = pl.ds(i * size, size)
        t_own[i] = dot3((ud_hi[rows, cols], ud_lo[rows, cols]), (hi[cols, cols], lo[cols, cols]), 0)
    fill_band(size, stages.at[1], oth_hi, oth_lo, -1, (2, 3))
    for case, rows in ((even, (4, 5)), (jnp.logical_not(even), (0, 1))):

        @pl.when(case)
        def _(rows=rows):
            fill_band(size, stages.at[1], oth_hi, oth_lo, -1, rows)


def product_rows(size, where, send, keeps, t_own, others, hi, lo, t_hi, t_lo):
    layer = where[1]
    for q in range(2):
        i = 2 * q + (1 - layer if send else layer)
        rows = pl.ds(aligned(q if send else q + layer, size), 4 * size)
        cols = pl.ds(aligned(q + 1 if send else q + layer, size), 4 * size)
        left = joined([others[i, m] for m in range(4)], 1)
        total = t_own[i] + dot3(left, (hi[rows, cols], lo[rows, cols]), 0)
        kept = [total[:, m * size : (m + 1) * size] * keeps[i, m, 0:1] for m in range(4)]
        t_hi[q], t_lo[q] = joined(kept, 1)


def product_send(size, where, keeps, t_own, ud_hi, ud_lo, hi_in, lo_in, u_cross, pc_z, t_hi, t_lo, ss, hi, lo):
    even, layer = where[0] % 2 == 0, where[1]
    for case, rows, first in ((even, (0, 1), 1), (jnp.logical_not(even), (4, 5), 16)):

        @pl.when(case)
        def _(rows=rows, first=first):
            fill_band(size, pc_z, hi, lo, -1, rows, first)

    product_rows(size, where, True, keeps, t_own, u_cross, hi, lo, t_hi, t_lo)
    for q in range(2):
        cols = pl.ds(aligned(q + 1 - layer, size), 4 * size)
        sums = dot3((t_hi[q], t_lo[q]), (ud_hi[:, cols], ud_lo[:, cols]), 1)
        for r in range(4):
            ss[q, r] = sums[:, r * size : (r + 1) * size]


def product_keep(size, where, keeps, t_own, hi, lo, u_cross, t_hi, t_lo):
    product_rows(size, where, False, keeps, t_own, u_cross, hi, lo, t_hi, t_lo)


def gather_halo(pieces, stage, sems):
    spots = [stage.at[pl.ds(at, n)] for at, n in (*PARTS, (16, 7), (23, 5))]
    return [start(x, spot, sems.at[n]) for n, (x, spot) in enumerate(zip(pieces, spots)) if x is not None]


def fill_halo(size, where, stage, uh_hi, uh_lo, rows, blocks):
    even, layer = where[0] % 2 == 0, where[1]
    for below_at, above_at, pack, case in ((16, 0, PACK[1], even), (0, 16, PACK[0], jnp.logical_not(even))):

        @pl.when(case)
        def _(below_at=below_at, above_at=above_at, pack=pack):
            for first, above in ((below_at, 0), (above_at, 1)):
                for n, (r, m) in enumerate(pack):
                    if first + n not in blocks or r not in rows or (above and r == 3):
                        continue
                    at = pl.ds((above * len(rows) + rows.index(r)) * size, size)
                    cols = pl.ds(aligned(slot_base(r, layer) + 4 * above + m, size), size)
                    uh_hi[at, cols], uh_lo[at, cols] = halves(stage[first + n])


def halo_sums(size, i, base, t_rows, uh_hi, uh_lo, ts=(0, 1, 2, 3)):
    cols = pl.ds(aligned(base + 2, size), 4 * size)
    rows = [pl.ds(aligned(jnp.where(t < i, len(ts) + n, n), size), size) for n, t in enumerate(ts)]
    hi = jnp.concatenate([uh_hi[r, cols] for r in rows], axis=0)
    lo = jnp.concatenate([uh_lo[r, cols] for r in rows], axis=0)
    return dot3(t_rows, (hi, lo), 1)


def send_sums(size, ts, where, t_hi, t_lo, uh_hi, uh_lo, out):
    for q in range(2):
        i, base = 2 * q + 1 - where[1], q + 1 - where[1]
        sums = halo_sums(size, i, base, (t_hi[q], t_lo[q]), uh_hi, uh_lo, ts)
        for n in range(len(ts)):
            out[q, n] = sums[:, n * size : (n + 1) * size]


def first_halo(size, where, y0, y1, z0, t_hi, t_lo, out, uh_hi, uh_lo, stage, sems):
    copies = gather_halo((y0, y1, z0), stage, sems)
    uh_hi[...] = jnp.zeros_like(uh_hi)
    uh_lo[...] = jnp.zeros_like(uh_lo)
    for c in copies:
        c.wait()
    fill_halo(size, where, stage, uh_hi, uh_lo, (0, 1), range(23))
    send_sums(size, (0, 1), where, t_hi, t_lo, uh_hi, uh_lo, out)


def halo_matrix(size, where, y0, y1, z0, uh_hi, uh_lo, stage, sems):
    copies = gather_halo((y0, y1, z0), stage, sems)
    uh_hi[...] = jnp.zeros_like(uh_hi)
    uh_lo[...] = jnp.zeros_like(uh_lo)
    for c in copies:
        c.wait()
    fill_halo(size, where, stage, uh_hi, uh_lo, (2, 3), range(23))


def last_halo(size, where, z1, t_hi, t_lo, hi_in, lo_in, out, uh_hi, uh_lo, stage, sems):
    for c in gather_halo((None, None, None, z1), stage, sems):
        c.wait()
    fill_halo(size, where, stage, uh_hi, uh_lo, (2, 3), range(23, 28))
    send_sums(size, (2, 3), where, t_hi, t_lo, uh_hi, uh_lo, out)


def out_keep(total_rows, where, o_mask, q, o):
    col = where[0] * 4 + 2 * q + where[1] - 4 + o
    return jnp.where((col >= 0) & (col < total_rows), o_mask[q, 0, o], 0).astype(F32)


def keep_rows(total_rows, size, where, o_mask, ss, halo, *refs):
    (t_hi, t_lo), (ud_hi, ud_lo), first, last = (refs[2 * n : 2 * n + 2] for n in range(4))
    out_any, part, keeps, out, sems = refs[8:]
    stores = []
    for q in range(2):
        i = 2 * q + where[1]
        t_rows = (t_hi[q], t_lo[q])
        cols = pl.ds(q * size, 4 * size)
        own = dot3(t_rows, (ud_hi[:, cols], ud_lo[:, cols]), 1)
        near = halo_sums(size, i, q, t_rows, *first, (0, 1))
        for n in range(6):
            o = (4 - i + n) % 8
            keep = out_keep(total_rows, where, o_mask, q, o)
            if n < 4:
                out[q, n] = (own[:, n * size : (n + 1) * size] + ss[q, n]) * keep
            else:
                out[q, n] = (near[:, (n - 4) * size : (n - 3) * size] + halo[q, n - 4]) * keep
            stores.append(start(out.at[q, n], out_any.at[q, 0, o], sems.at[6 * q + n]))
        sums = halo_sums(size, i, q, t_rows, *last, (2, 3))
        for n in range(2):
            keep = out_keep(total_rows, where, o_mask, q, (10 - i + n) % 8)
            part[q, n] = sums[:, n * size : (n + 1) * size] * keep
            keeps[q, n] = jnp.full(keeps.shape[2:], keep, F32)
    for c in stores:
        c.wait()


def combine(where, keeps, part, halo, kept_any, out_any, out, sems):
    stores = []
    for q in range(2):
        for n in range(2):
            o = (10 - 2 * q - where[1] + n) % 8
            out[q, n] = part[q, n] + halo[q, n] * keeps[q, n, 0:1]
            stores.append(start(out.at[q, n], out_any.at[q, 0, o], sems.at[2 * q + n]))
    for c in stores:
        c.wait()


def after(x, *others):
    return lax.optimization_barrier((x, *others))[0]


def on_device(u_values, u_mask, p_values, p_mask, t_mask, out_mask):
    size = u_values.shape[-1]
    slabs = lax.axis_size(SLABS)
    total_rows = slabs * u_values.shape[0]
    swap = [(0, 1), (1, 0)]
    pair = [(s, s ^ 1) for s in range(slabs)]
    onward = [(s, s + 2) for s in range(0, slabs - 2, 2)] + [(s, s - 2) for s in range(3, slabs, 2)]

    def over_layer(x):
        return lax.ppermute(x, "layer", swap)

    def over_pair(x):
        return lax.ppermute(x, SLABS, pair)

    def onto(x):
        return lax.ppermute(x, SLABS, onward)

    def sems(n):
        return pltpu.SemaphoreType.DMA((n,))

    eight = shape(2, 4, size, size)
    wide = 6 * size
    unit = 3 * 2 * (4 * size) ** 2 * size
    po, pe = call(
        keep_p,
        [vmem(8, size, size)] * 2,
        [HBM, HBM],
        [pltpu.SMEM(p_mask.shape, jnp.int32), vmem(*p_values.shape), sems(3)],
    )(p_mask, p_values)
    pc = over_layer(po)
    pe_y = over_pair(pe)
    u_mask, t_mask = u_mask[:, :, 0], t_mask[:, :, 0]
    u_own, *packed = call(
        keep_u,
        [shape(4, 4, size, size)] + [shape(n, size, size) for _, n in PARTS],
        [HBM, HBM],
        [pltpu.SMEM(u_mask.shape, jnp.int32), vmem(*u_values.shape), vmem(4, 4, size, size)]
        + [vmem(16, size, size), sems(11)],
    )(u_mask, u_values)
    u_oth = over_layer(after(u_own, pc))
    pe_z = onto(after(pe_y[:7], u_own))
    pc_y = over_pair(after(pc, u_own))
    pc_z = onto(pc_y[:7])
    t_like = (4, size, 4 * size)
    band = [vmem(wide, wide, dtype=BF16)] * 2
    own_rows = [vmem(4 * size, wide, dtype=BF16)] * 2
    t_own, ud_hi, ud_lo, *oth, keeps = call(
        functools.partial(product_own, total_rows, size),
        [vmem(*t_like), *own_rows, *band, vmem(4, 4, 8, size)],
        [HBM, HBM, HBM, HBM, ANY] + [HBM] * 3,
        [pltpu.SMEM(x.shape, jnp.int32) for x in (p_mask, t_mask)]
        + [vmem(*p_values.shape)]
        + [vmem(2, 24, size, size), vmem(4, 4, size, size), *band, sems(11)],
        flops=22 * unit,
    )(u_own, p_mask, p_values, t_mask, pe_z, pe_y, pc, pc_y)
    u_y = [over_pair(after(x, pc)) for x in packed]
    u_z = [onto(after(u_y[0], t_own))]
    rows = [vmem(2, size, 4 * size, dtype=BF16)] * 2
    *t_send, ss, hi, lo = call(
        functools.partial(product_send, size),
        [*rows, vmem(2, 4, size, size), *band],
        [VMEM] * 8,
        flops=4 * unit,
        alias={4: 3, 5: 4},
    )(keeps, t_own, ud_hi, ud_lo, *oth, u_oth, pc_z)
    ss_got = over_layer(ss)
    t_keep = call(
        functools.partial(product_keep, size),
        rows,
        [VMEM] * 5,
        flops=2 * unit,
    )(keeps, t_own, hi, lo, u_oth)
    u_z.append(onto(after(u_y[1][:5], t_send[0])))
    uh = [vmem(4 * size, 9 * size, dtype=BF16)] * 2
    pair_sums = vmem(2, 2, size, size)
    stage = vmem(28, size, size)
    halo, *uh_first = call(
        functools.partial(first_halo, size),
        [pair_sums, *uh],
        [HBM, ANY, ANY, VMEM, VMEM],
        [stage, sems(3)],
        flops=unit,
    )(*u_y, u_z[0], *t_send)
    halo_got = over_layer(halo)
    uh_last = call(functools.partial(halo_matrix, size), uh, [HBM, ANY, ANY], [stage, sems(3)])(
        after(u_y[0], halo), u_y[1], u_z[0]
    )
    last, *uh_last = call(
        functools.partial(last_halo, size),
        [pair_sums, *uh],
        [ANY] + [VMEM] * 4,
        [stage, sems(4)],
        flops=unit,
        alias={3: 1, 4: 2},
    )(u_z[1], *t_send, *uh_last)
    last_got = over_layer(last)
    kept, part, keeps = call(
        functools.partial(keep_rows, total_rows, size),
        [shape(*p_values.shape), pair_sums, vmem(2, 2, 8, size)],
        [SMEM] + [VMEM] * 10,
        [vmem(2, 6, size, size), sems(12)],
        flops=40 * unit,
    )(out_mask, ss_got, halo_got, *t_keep, ud_hi, ud_lo, *uh_first, *uh_last)
    (out,) = call(
        combine,
        [shape(*p_values.shape)],
        [VMEM, VMEM, VMEM, ANY],
        [vmem(2, 2, size, size), sems(4)],
        alias={3: 0},
        limit=16,
    )(keeps, part, last_got, kept)
    return out


def solution(mesh):
    placed = (
        P(SLABS, None, "layer", None, None),
        P(SLABS, None, "layer"),
        P(SLABS, "layer", None, None, None),
        P(SLABS, "layer", None),
        P(SLABS, None, "layer"),
        P(SLABS, "layer", None),
    )
    return jax.shard_map(
        on_device,
        mesh=mesh,
        in_specs=placed,
        out_specs=P(SLABS, "layer", None, None, None),
        check_vma=False,
    )
```
